256 devices in a mesh: seq: 32 (over z, y), head: 8 (over x, core).
Axes of the slice: x: 4, y: 4, z: 8, core: 2. Of those that a mesh axis runs over, the one named last changes fastest.
Arguments:
- lengths: int32 [32], replicated, may hold values from 1 to 16384, as said below
- block_table: int32 [32, 256], replicated, may hold values from 0 to 2047, as said below
- slot_request: int32 [32], replicated, may hold values from 0 to 31, each once
- kv_pool: bfloat16 [2048, 64, 8, 256], P('seq', None, 'head'), may hold values from -4 to 4
- new_kv: bfloat16 [3, 32, 8, 256], P(None, 'seq', 'head'), may hold values from -4 to 4
- queries: bfloat16 [2, 32, 8, 1024], P(None, 'seq', 'head'), may hold values from -20 to 20
- residual: bfloat16 [2, 32, 16384], P(None, None, 'seq'), may hold values from -32 to 32
- norm_gain: float32 [16384], P('seq'), may hold values from 0.1 to 1.9
- w_out: bfloat16 [8, 1024, 16384], P('head', None, 'seq'), may hold values from -0.0625 to 0.0625
- w_gate: bfloat16 [26624, 16384], P(('seq', 'head')), may hold values from -0.046875 to 0.046875
- w_up: bfloat16 [26624, 16384], P(('seq', 'head')), may hold values from -0.046875 to 0.046875
- w_down: bfloat16 [26624, 16384], P(('seq', 'head')), may hold values from -0.15625 to 0.15625
Outputs:
- layer_out: bfloat16 [2, 32, 16384], P(None, None, ('seq', 'head'))
The draws below stay inside these ranges and needn't reach their ends.
Inputs may be any that keep to these rules, and one draw needn't show every extreme that they name: `lengths`: the longest request has exactly 16384 tokens; the pages of all requests together number 2048. `block_table`: for j below request r's page count, entry [r, j] is the pool slot of its page j. Numbering the pages of all requests in order (request r's pages start at O_r, the pages of the requests before r), page O_r + j lies on shard (O_r + j) mod 32, that is in a slot from ((O_r + j) mod 32) * 64 on; every slot holds one page; within a shard the slots are in no order. Entries past the page count are 0.
All inputs are finite; a program needn't handle non-finite values.
Results may differ from the reference program's by a relative error of at most 0.012.
Values may be sent and summed in bfloat16 or wider, within the bound.
A program may use at most 128 MiB of HBM per device.

```python
import math
import jax
import jax.numpy as jnp
from jax import lax

D = 16384
FF = 26624
HEAD_DIM = 128
GROUP = 8
KV_HEADS = 8
PAGE = 64
STEPS = 2
NEW = 3
REQUESTS = 32
PAGES_SHARD = 8
REQUEST_PAGE_CAP = 256
SLOTS_DEV = 64
SLOTS = 2048


def page_layout(key):
    key = jax.random.fold_in(key, 101)
    weight_key, order_key, tail_key, shuffle_key = jax.random.split(key, 4)
    shard_count = REQUEST_PAGE_CAP // PAGES_SHARD
    spare_pages = SLOTS - REQUEST_PAGE_CAP - (REQUESTS - 1)
    powers = jax.random.randint(weight_key, (REQUESTS,), 0, 6)
    weights = jnp.left_shift(jnp.ones((REQUESTS,), jnp.int32), powers)
    weights = weights.at[0].set(0)
    page_portions = jnp.minimum(spare_pages * weights // jnp.sum(weights), REQUEST_PAGE_CAP - 1)
    unassigned_pages = spare_pages - jnp.sum(page_portions)
    remaining_capacity = (REQUEST_PAGE_CAP - 1 - page_portions).at[0].set(0)
    prior_page_counts = jnp.cumsum(remaining_capacity) - remaining_capacity
    extra_page_grant = jnp.clip(unassigned_pages - prior_page_counts, 0, remaining_capacity)
    sorted_requests = (1 + page_portions + extra_page_grant).at[0].set(REQUEST_PAGE_CAP)
    placing = jax.random.permutation(order_key, REQUESTS)
    page_count = jnp.zeros((REQUESTS,), jnp.int32).at[placing].set(sorted_requests.astype(jnp.int32))
    last_fill = jax.random.randint(tail_key, (REQUESTS,), 1, PAGE + 1)
    last_fill = last_fill.at[placing[0]].set(PAGE)
    token_count = (page_count - 1) * PAGE + last_fill
    offsets = jnp.cumsum(page_count) - page_count
    page_index = jnp.arange(REQUEST_PAGE_CAP, dtype=jnp.int32)
    logical = offsets[:, None] + page_index[None, :]
    inside = page_index[None, :] < page_count[:, None]
    owner_shard = logical % shard_count
    within = jnp.clip(logical // shard_count, 0, SLOTS_DEV - 1)
    shuffles = jax.vmap(lambda part_key: jax.random.permutation(part_key, SLOTS_DEV))(jax.random.split(shuffle_key, shard_count))
    slot_index = owner_shard * SLOTS_DEV + shuffles[owner_shard, within]
    page_table = jnp.where(inside, slot_index, 0)
    return (token_count.astype(jnp.int32), page_table.astype(jnp.int32))


def draw_lengths(key, part):
    token_count, page_table = page_layout(key)
    return token_count


def draw_block_table(key, part):
    token_count, page_table = page_layout(key)
    return page_table


def draw_new_kv(key, part):
    key = jax.random.fold_in(key, 5)
    values = jnp.clip(jax.random.normal(key, (NEW, REQUESTS, KV_HEADS, 2 * HEAD_DIM), jnp.float32), -4.0, 4.0)
    return values.astype(jnp.bfloat16)


def draw_queries(key, part):
    key = jax.random.fold_in(key, 7)
    values = jnp.clip(jax.random.normal(key, (STEPS, REQUESTS, KV_HEADS, GROUP * HEAD_DIM), jnp.float32), -4.0, 4.0)
    return values.astype(jnp.bfloat16)


def draw_residual(key, part):
    key = jax.random.fold_in(key, 21)
    row_key, spread_key, value_key = jax.random.split(key, 3)
    position = jnp.arange(D, dtype=jnp.float32) / D - 0.5
    row_scale = jnp.exp(jax.random.uniform(row_key, (STEPS, REQUESTS, 1), jnp.float32, math.log(0.3), math.log(3.0)))
    column_scale = jnp.exp(jax.random.uniform(spread_key, (D,), jnp.float32, math.log(0.15), math.log(1.5))) * 3.0 ** position
    values = jnp.clip(jax.random.normal(value_key, (STEPS, REQUESTS, D), jnp.float32), -4.0, 4.0)
    return (values * row_scale * column_scale).astype(jnp.bfloat16)


def raised(drawn, rng, source, target, blocks, factor):
    owner, partner = [(jnp.arange(drawn.shape[dim]) // (drawn.shape[dim] // blocks)).reshape([-1 if axis == dim else 1 for axis in range(drawn.ndim)]) for dim in (source, target)]
    chosen = jax.random.permutation(rng, blocks)[partner]
    strong = (owner == chosen) | (owner == (partner + blocks // 2) % blocks)
    return jnp.where(strong, factor * drawn, drawn)


def level_of(own_key, shape, cuts, least, high):
    level = 1.0
    for axis_at, parts in cuts:
        heights = jax.random.uniform(jax.random.fold_in(jax.random.fold_in(own_key, 6), axis_at), (parts,), jnp.float32, least / len(cuts), high / len(cuts))
        level = level * jnp.repeat(jnp.exp(heights), shape[axis_at] // parts).reshape((-1,) + (1,) * (len(shape) - 1 - axis_at))
    return level


def centred(stream_key, shape, width, limit, cuts=(), kind=jnp.bfloat16):
    entries = width * jax.random.normal(stream_key, shape, jnp.float32)
    if cuts:
        entries = entries * level_of(stream_key, shape, cuts, -0.22, 0.18)
    return jnp.clip(entries, -limit, limit).astype(kind)


def noise_with(own_key, extent, scale, bound, pieces, heavy, held_as=jnp.bfloat16):
    drawn = scale * jax.random.normal(own_key, extent, jnp.float32)
    if pieces:
        drawn = drawn * level_of(own_key, extent, pieces, -0.22, 0.18)
    return jnp.clip(raised(drawn, jax.random.fold_in(own_key, 3), *heavy), -bound, bound).astype(held_as)


def setup_inputs(seed: int = 0) -> dict:
    seeds = jax.random.split(jax.random.key(seed), 13)
    return {
        "lengths": draw_lengths(jax.random.fold_in(seeds[12], 71), 0),
        "block_table": draw_block_table(jax.random.fold_in(seeds[12], 71), 0),
        "slot_request": jax.random.permutation(seeds[2], REQUESTS).astype(jnp.int32),
        "kv_pool": centred(seeds[3], (SLOTS, PAGE, KV_HEADS, 2 * HEAD_DIM), 1.0, 4.0, ((0, 32), (2, 8))),
        "new_kv": draw_new_kv(jax.random.fold_in(seeds[12], 71), 0),
        "queries": draw_queries(jax.random.fold_in(seeds[12], 71), 0),
        "residual": draw_residual(jax.random.fold_in(seeds[12], 71), 0),
        "norm_gain": jnp.clip(1.0 + 0.18 * jax.random.normal(seeds[7], (D,), jnp.float32), 0.1, 1.9),
        "w_out": centred(seeds[8], (KV_HEADS, GROUP * HEAD_DIM, D), (KV_HEADS * GROUP * HEAD_DIM) ** -0.5, 0.0625, ((0, 8), (2, 32))),
        "w_gate": centred(seeds[9], (FF, D), D ** -0.5, 0.046875, ((0, 256),)),
        "w_up": centred(seeds[10], (FF, D), D ** -0.5, 0.046875, ((0, 256),)),
        "w_down": noise_with(seeds[11], (FF, D), FF ** -0.5, 0.15625, ((0, 256),), (0, 1, 256, 6.0)),
    }


def reference(lengths, block_table, slot_request, kv_pool, new_kv, queries, residual, norm_gain, w_out, w_gate, w_up, w_down):
    positions = jnp.arange(REQUEST_PAGE_CAP * PAGE, dtype=jnp.int32)
    fresh_mask = jnp.arange(NEW)[None, :] <= jnp.arange(STEPS)[:, None] + 1
    score_scale = 1.0 / math.sqrt(HEAD_DIM)

    def attend(items):
        table_row, length_here, query_here, fresh_here = items
        cached = kv_pool[table_row].reshape(REQUEST_PAGE_CAP * PAGE, KV_HEADS, 2 * HEAD_DIM)
        keys_all = jnp.concatenate([cached[:, :, :HEAD_DIM], fresh_here[:, :, :HEAD_DIM]], 0).astype(jnp.float32)
        values_all = jnp.concatenate([cached[:, :, HEAD_DIM:], fresh_here[:, :, HEAD_DIM:]], 0).astype(jnp.float32)
        grouped = query_here.reshape(STEPS, KV_HEADS, GROUP, HEAD_DIM).astype(jnp.float32)
        scores = jnp.einsum('tkgd,nkd->tkgn', grouped, keys_all) * score_scale
        in_cache = jnp.broadcast_to((positions < length_here)[None, :], (STEPS, REQUEST_PAGE_CAP * PAGE))
        valid_keys = jnp.concatenate([in_cache, fresh_mask], 1)
        scores = jnp.where(valid_keys[:, None, None, :], scores, -jnp.inf)
        row_peak = lax.optimization_barrier(jnp.max(scores, -1, keepdims=True))
        weights = jnp.exp(scores - row_peak).astype(jnp.bfloat16)
        weights = lax.optimization_barrier(weights).astype(jnp.float32)
        weight_sum = lax.optimization_barrier(jnp.sum(weights, -1, keepdims=True))
        mixed_values = jnp.einsum('tkgn,nkd->tkgd', weights, values_all) / weight_sum
        return mixed_values.astype(jnp.bfloat16).reshape(STEPS, KV_HEADS, GROUP * HEAD_DIM)
    items = (block_table[slot_request], lengths[slot_request], queries.transpose(1, 0, 2, 3), new_kv.transpose(1, 0, 2, 3))
    attended = lax.map(attend, items)
    flat_heads = attended.transpose(1, 0, 2, 3).reshape(STEPS * REQUESTS, KV_HEADS * GROUP * HEAD_DIM)
    projected = jnp.dot(flat_heads, w_out.reshape(KV_HEADS * GROUP * HEAD_DIM, D), preferred_element_type=jnp.float32)
    hidden_state = residual.reshape(STEPS * REQUESTS, D).astype(jnp.float32) + projected
    mean_square = lax.optimization_barrier(jnp.mean(hidden_state * hidden_state, -1, keepdims=True))
    normed = (hidden_state * lax.rsqrt(mean_square + 1e-05) * norm_gain).astype(jnp.bfloat16)
    gate_sum = jnp.dot(normed, w_gate.T, preferred_element_type=jnp.float32)
    up_sum = jnp.dot(normed, w_up.T, preferred_element_type=jnp.float32)
    activation = (jax.nn.silu(gate_sum) * up_sum).astype(jnp.bfloat16)
    mlp_sum = jnp.dot(activation, w_down, preferred_element_type=jnp.float32)
    return (hidden_state + mlp_sum).astype(jnp.bfloat16).reshape(STEPS, REQUESTS, D)
```

```python
import math

import jax
import jax.numpy as jnp
from jax import lax
from jax.experimental import pallas as pl
from jax.experimental.pallas import tpu as pltpu
from jax.sharding import PartitionSpec as P

EPSILON = 1e-05
NZ, NY, NX, NC = 8, 4, 4, 2
NS, NH = NZ * NY, NX * NC
HD = 128
PAGE = 64
ROWS = 16
TOKENS = 4096
CHUNK = 256
FAR = 131072.0
F32, BF16 = jnp.float32, jnp.bfloat16
NT = (((1,), (1,)), ((), ()))
EXP_SCALE = math.log2(math.e) / math.sqrt(HD)


def iota(shape, dim):
    return lax.broadcasted_iota(jnp.int32, shape, dim)


def stat_tile(total):
    high = total.astype(BF16).astype(F32)
    row = iota((16, HD), 0)
    tile = jnp.where(row == 0, high, jnp.where(row == 1, total - high, 0.0))
    return tile.astype(BF16)


def kernel(
    lengths, slot_request, table, new_kv, queries, residual, gain,
    kv_hbm, wo_hbm, wg_hbm, wu_hbm, wd_hbm,
    out,
    kv, bias, wo, wg, wu, wd,
    qall, hot, codes, scores, peak, acc,
    ps, pr, ag, af, hp, hr, hid,
    zb, x1, y2, y1, x2, py1, px2,
    o1, o2, sb, rb, s1, r1, s2, rx2,
    t1f, t1b, rt1, t2f, t2b, rt2, us, ur,
    load_sem, snd, rcv, y_sem, x_sem, rb_sem,
):
    s = lax.axis_index("seq")
    h = lax.axis_index("head")
    z, y = s // NY, s % NY
    x, c = h // NC, h % NC
    partner = (s, x * NC + 1 - c)

    def at_y(other):
        return (z * NY + other, h)

    def at_x(other):
        return (s, other * NC + c)

    def send(src, dst, send_sem, recv_sem, device):
        pltpu.make_async_remote_copy(
            src_ref=src,
            dst_ref=dst,
            send_sem=send_sem,
            recv_sem=recv_sem,
            device_id=device,
            device_id_type=pl.DeviceIdType.MESH,
        ).start()

    def settle(like, sem):
        pltpu.make_async_copy(like, like, sem).wait()

    loads = [
        pltpu.make_async_copy(src, dst, load_sem.at[n])
        for n, (src, dst) in enumerate(
            ((kv_hbm, kv), (wo_hbm, wo), (wg_hbm, wg), (wu_hbm, wu), (wd_hbm, wd))
        )
    ]
    for load in loads:
        load.start()

    barrier = pltpu.get_barrier_semaphore()

    def greet(device):
        pl.semaphore_signal(barrier, inc=1, device_id=device, device_id_type=pl.DeviceIdType.MESH)

    @pl.loop(1, NS)
    def _(d):
        greet(((s + d) % NS, h))

    @pl.loop(1, NH)
    def _(d):
        greet((s, (h + d) % NH))

    @pl.loop(1, NZ)
    def _(d):
        greet((((z + d) % NZ) * NY + y, x * NC + 1 - c))

    row = iota((NS, HD), 0)
    length = jnp.zeros((NS, HD), jnp.int32)
    slot = jnp.zeros((NS, HD), jnp.int32)
    for r in range(NS):
        length = jnp.where(row == r, lengths[r], length)
        slot = jnp.where(row == slot_request[r], r, slot)
    halves = []
    for half in range(2):
        page = iota((NS, HD), 1) + half * HD
        filled = jnp.clip(length - page * PAGE, 0, PAGE)
        local = jnp.where(filled > 0, table[:, half * HD : (half + 1) * HD] - s * PAGE, -1)
        halves.append((local, (slot * HD + filled).astype(F32)))

    def find(p, carry):
        hits = [jnp.where(local == p, code, 0.0) for local, code in halves]
        codes[pl.ds(p, 1), :] = jnp.sum(hits[0] + hits[1], axis=0, keepdims=True)
        return carry

    lax.fori_loop(0, PAGE, find, 0)
    code = jnp.sum(codes[...], axis=1, keepdims=True)
    codes[...] = jnp.broadcast_to(code, (PAGE, HD))

    def cover(p, carry):
        both = codes[pl.ds(p, 1), :].astype(jnp.int32)
        mine = (iota((PAGE, HD), 1) == both // HD) & (iota((PAGE, HD), 0) < both % HD)
        bias[pl.ds(pl.multiple_of(p * PAGE, PAGE), PAGE), :] = jnp.where(mine, 0.0, -FAR).astype(BF16)
        return carry

    lax.fori_loop(0, PAGE, cover, 0)
    hot[...] = jnp.where(iota((NS * ROWS, HD), 0) // ROWS == iota((NS * ROWS, HD), 1), 1.0, 0.0).astype(BF16)

    wide = queries[...].astype(F32)
    own_query = jnp.concatenate(
        [wide[t : t + 1, g * HD : (g + 1) * HD] for t in range(2) for g in range(8)], axis=0
    )
    qall[s] = own_query.astype(BF16)

    pl.semaphore_wait(barrier, (NS - 1) + (NH - 1) + (NZ - 1))

    @pl.loop(1, NS)
    def _(d):
        send(qall.at[s], qall.at[s], snd.at[0], rcv.at[0], ((s + d) % NS, h))

    loads[0].wait()
    settle(qall.at[pl.ds(0, NS - 1)], rcv.at[0])

    aug_query = jnp.concatenate([qall[...].reshape(NS * ROWS, HD), hot[...]], axis=1)
    peak[...] = jnp.full((NS * ROWS, HD), -4.0 * FAR, F32)

    def score(k, carry):
        tokens = pl.ds(pl.multiple_of(k * CHUNK, CHUNK), CHUNK)
        aug_key = jnp.concatenate([kv[tokens, :HD], bias[tokens, :]], axis=1)
        raw = lax.dot_general(aug_query, aug_key, NT, preferred_element_type=F32)
        scores[:, tokens] = raw
        peak[...] = jnp.maximum(peak[...], jnp.maximum(raw[:, :HD], raw[:, HD:]))
        return carry

    lax.fori_loop(0, TOKENS // CHUNK, score, 0)
    top = jnp.max(peak[...], axis=1, keepdims=True).astype(BF16).astype(F32)
    peak[...] = jnp.broadcast_to(top, (NS * ROWS, HD))
    acc[...] = jnp.zeros((NS * ROWS, 2 * HD), F32)

    def mix(k, carry):
        tokens = pl.ds(pl.multiple_of(k * CHUNK, CHUNK), CHUNK)
        aug_value = jnp.concatenate([kv[tokens, HD:], jnp.ones((CHUNK, HD), BF16)], axis=1)
        base = jnp.concatenate([peak[...], peak[...]], axis=1)
        weights = jnp.exp2((scores[:, tokens] - base) * EXP_SCALE).astype(BF16)
        acc[...] += jnp.dot(weights, aug_value, preferred_element_type=F32)
        return carry

    lax.fori_loop(0, TOKENS // CHUNK, mix, 0)
    total = acc[:, HD:]
    high = total.astype(BF16).astype(F32)
    lane = iota((NS * ROWS, HD), 1)
    stats = jnp.where(lane == 0, peak[...], jnp.where(lane == 1, high, total - high))
    ps[:, :ROWS, :] = acc[:, :HD].astype(BF16).reshape(NS, ROWS, HD)
    ps[:, ROWS:, :] = stats.astype(BF16).reshape(NS, ROWS, HD)
    pr[s] = ps[s]

    @pl.loop(1, NS)
    def _(d):
        other = (s + d) % NS
        send(ps.at[other], pr.at[s], snd.at[1], rcv.at[1], (other, h))

    fresh = new_kv[...].astype(F32)
    late = iota((ROWS, 1), 0) >= ROWS // 2
    rounded_query = own_query.astype(BF16).astype(F32)
    fresh_scores = []
    for e in range(3):
        raw = jnp.sum(rounded_query * fresh[e : e + 1, :HD], axis=1, keepdims=True)
        fresh_scores.append(jnp.where(late, raw, -FAR) if e == 2 else raw)
    settle(pr.at[pl.ds(0, NS - 1)], rcv.at[1])
    stats = pr[:, ROWS:, :].astype(F32)
    tops = stats[:, :, 0:1]
    top = jnp.max(tops, axis=0)
    for raw in fresh_scores:
        top = jnp.maximum(top, raw)
    factor = jnp.exp2((tops - top[None]) * EXP_SCALE)
    total = jnp.sum(factor * (stats[:, :, 1:2] + stats[:, :, 2:3]), axis=0)
    mixed = jnp.sum(factor * pr[:, :ROWS, :].astype(F32), axis=0)
    for e, raw in enumerate(fresh_scores):
        weight = jnp.exp2((raw - top) * EXP_SCALE).astype(BF16).astype(F32)
        total = total + weight
        mixed = mixed + weight * fresh[e : e + 1, HD:]
    ag[s] = (mixed / total).astype(BF16)

    @pl.loop(1, NS)
    def _(d):
        send(ag.at[s], ag.at[s], snd.at[2], rcv.at[2], ((s + d) % NS, h))

    loads[1].wait()
    settle(ag.at[pl.ds(0, NS - 1)], rcv.at[2])

    af[...] = ag[...].reshape(NS * ROWS, HD).astype(F32)
    attended = jnp.concatenate(
        [
            jnp.concatenate([af[pl.ds(t * 8 + g, NS, stride=ROWS), :] for g in range(8)], axis=1)
            for t in range(2)
        ],
        axis=0,
    ).astype(BF16)
    part = jnp.dot(attended, wo[...], preferred_element_type=F32)
    for xx in range(NX):
        for cc in range(NC):
            hp[xx * NC + cc] = part[cc * NS : (cc + 1) * NS, xx * HD : (xx + 1) * HD]
    hr[h] = hp[h]

    @pl.loop(1, NH)
    def _(d):
        other = (h + d) % NH
        send(hp.at[other], hr.at[h], snd.at[3], rcv.at[3], (s, other))

    columns = pl.ds(pl.multiple_of(x * HD, HD), HD)
    settle(hr.at[pl.ds(0, NH - 1)], rcv.at[3])
    hidden = residual[c, :, columns].astype(F32) + jnp.sum(hr[...], axis=0)
    hid[c] = hidden
    square = jnp.sum(hidden * hidden, axis=1, keepdims=True)
    spread = jnp.where(iota((NS, HD), 0) == iota((NS, HD), 1), square, 0.0)
    zb[z, 0:32] = (hidden * gain[:, columns]).astype(BF16)
    zb[z, 32:48] = stat_tile(jnp.sum(spread, axis=0, keepdims=True))

    @pl.loop(1, NZ)
    def _(d):
        send(zb.at[z], zb.at[z], snd.at[4], rcv.at[4], (((z + d) % NZ) * NY + y, h))

    send(hid.at[c], hid.at[c], snd.at[5], rcv.at[5], partner)
    settle(zb.at[pl.ds(0, NZ - 1)], rcv.at[4])
    x1[x, 0:128] = zb[:, 0:16, :].reshape(128, HD)
    stats = jnp.sum(zb[:, 32:48, :].astype(F32), axis=0)
    x1[x, 128:144] = stat_tile(stats[0:1] + stats[1:2])
    y2[y] = zb[:, 16:32, :].reshape(128, HD)
    for d in range(1, 4):
        send(x1.at[x], x1.at[x], snd.at[6], rcv.at[6], at_x((x + d) % NX))
        send(y2.at[y], y2.at[y], snd.at[7], rcv.at[7], at_y((y + d) % NY))
    settle(x1.at[pl.ds(0, 3)], rcv.at[6])
    for xx in range(NX):
        y1[y, xx * 128 : (xx + 1) * 128] = x1[xx, 0:128]
    stats = jnp.sum(x1[:, 128:144, :].astype(F32), axis=0)
    y1[y, 512:528] = stat_tile(stats[0:1] + stats[1:2])
    for d in range(1, 4):
        send(y1.at[y], y1.at[y], snd.at[8], y_sem.at[d - 1], at_y((y + d) % NY))
    send(y1.at[y], py1.at[y], snd.at[10], rcv.at[8], partner)
    settle(y2.at[pl.ds(0, 3)], rcv.at[7])
    for yy in range(NY):
        x2[x, yy * 128 : (yy + 1) * 128] = y2[yy]
    for d in range(1, 4):
        send(x2.at[x], x2.at[x], snd.at[9], x_sem.at[d - 1], at_x((x + d) % NX))
    send(x2.at[x], px2.at[x], snd.at[11], rcv.at[9], partner)
    for d in range(1, 4):
        origin = (y + NY - d) % NY
        settle(y1.at[origin], y_sem.at[d - 1])
        send(y1.at[origin], py1.at[origin], snd.at[10], rcv.at[8], partner)
        origin = (x + NX - d) % NX
        settle(x2.at[origin], x_sem.at[d - 1])
        send(x2.at[origin], px2.at[origin], snd.at[11], rcv.at[9], partner)
    loads[2].wait()
    loads[3].wait()
    settle(py1, rcv.at[8])
    settle(px2, rcv.at[9])

    def gate_up(n, carry):
        gate, up = carry
        yy, xp = n // 2, n % 2
        for zz in range(NZ):
            pieces = []
            for first, second in ((y1, x2), (py1, px2)):
                pieces.append(
                    jnp.concatenate(
                        [
                            first[yy, pl.ds(pl.multiple_of((xp * 2 + e) * 128 + zz * 16, 16), 16), :]
                            for e in range(2)
                        ],
                        axis=1,
                    )
                )
                pieces.append(
                    jnp.concatenate(
                        [
                            second[xp * 2 + e, pl.ds(pl.multiple_of(yy * 128 + zz * 16, 16), 16), :]
                            for e in range(2)
                        ],
                        axis=1,
                    )
                )
            stream = jnp.concatenate(pieces, axis=0)
            where = pl.ds(pl.multiple_of(zz * 2048 + yy * 512 + xp * 256, 256), 256)
            gate = gate + lax.dot_general(stream, wg[:, where], NT, preferred_element_type=F32)
            up = up + lax.dot_general(stream, wu[:, where], NT, preferred_element_type=F32)
        return gate, up

    zero = jnp.zeros((64, 104), F32)
    gate, up = lax.fori_loop(0, 8, gate_up, (zero, zero))
    own_stats = jnp.sum(y1[:, 512:528, :].astype(F32), axis=0)
    other_stats = jnp.sum(py1[:, 512:528, :].astype(F32), axis=0)
    square = jnp.concatenate(
        [
            jnp.sum(
                jnp.where(iota((NS, HD), 0) == iota((NS, HD), 1), tile[0:1] + tile[1:2], 0.0),
                axis=1,
                keepdims=True,
            )
            for tile in (own_stats, other_stats)
        ],
        axis=0,
    )
    scale = lax.rsqrt(square * (1.0 / 16384.0) + EPSILON)
    gate = gate * scale
    up = up * scale
    activation = (gate / (1.0 + jnp.exp(-gate)) * up).astype(BF16)

    loads[4].wait()

    def down(k):
        yy = (y + k + 1) % NY

        def body(xp, carry):
            for zz in range(NZ):
                where = pl.ds(pl.multiple_of(zz * 2048 + yy * 512 + xp * 256, 256), 256)
                block = jnp.dot(activation, wd[:, where], preferred_element_type=F32)
                for e in range(2):
                    piece = block[:, e * HD : (e + 1) * HD]
                    at = pl.multiple_of((xp * 2 + e) * 128 + zz * 16, 16)
                    o1[k, pl.ds(at, 16), :] = piece[0:16]
                    o2[k, pl.ds(at, 16), :] = piece[16:32]
                    sb[k, pl.ds(at, 16), :] = piece[32:48].astype(BF16)
                    sb[k, pl.ds(at + 512, 16), :] = piece[48:64].astype(BF16)
            return carry

        lax.fori_loop(0, 2, body, 0)
        send(sb.at[k], rb.at[k], snd.at[12], rb_sem.at[k], partner)

    def finish(k):
        yy = (y + k + 1) % NY
        settle(rb.at[k], rb_sem.at[k])
        first = o1[k] + rb[k, 0:512].astype(F32)
        if k < 3:
            s1[k] = first.astype(BF16)
            send(s1.at[k], r1.at[k], snd.at[13], rcv.at[10], at_y(yy))
        else:
            o1[k] = first
        second = o2[k] + rb[k, 512:1024].astype(F32)
        o2[k] = second
        for xx in range(NX):
            s2[xx, pl.ds(pl.multiple_of(yy * 128, 128), 128), :] = second[xx * 128 : (xx + 1) * 128].astype(BF16)

    for k in range(4):
        down(k)
        if k > 0:
            finish(k - 1)
    finish(3)
    for j in range(3):
        other = (x + j + 1) % NX
        send(s2.at[other], rx2.at[j], snd.at[14], rcv.at[11], at_x(other))

    settle(r1, rcv.at[10])
    whole = o1[3]
    for j in range(3):
        whole = whole + r1[j].astype(F32)
    t1f[...] = whole.reshape(NX, 128, HD)
    t1b[...] = whole.reshape(NX, 128, HD).astype(BF16)
    for j in range(3):
        other = (x + j + 1) % NX
        send(t1b.at[other], rt1.at[j], snd.at[15], rcv.at[12], at_x(other))

    settle(rx2, rcv.at[11])
    for k in range(4):
        yy = (y + k + 1) % NY
        rows = pl.ds(pl.multiple_of(yy * 128, 128), 128)
        whole = o2[k, pl.ds(pl.multiple_of(x * 128, 128), 128), :]
        for j in range(3):
            whole = whole + rx2[j, rows, :].astype(F32)
        if k < 3:
            t2b[k] = whole.astype(BF16)
            send(t2b.at[k], rt2.at[k], snd.at[16], rcv.at[13], at_y(yy))
        else:
            t2f[...] = whole

    settle(rt1, rcv.at[12])
    whole = t1f[x]
    for j in range(3):
        whole = whole + rt1[j].astype(F32)
    us[:, 0:16, :] = whole.reshape(NZ, 16, HD).astype(BF16)
    settle(rt2, rcv.at[13])
    whole = t2f[...]
    for j in range(3):
        whole = whole + rt2[j].astype(F32)
    us[:, 16:32, :] = whole.reshape(NZ, 16, HD).astype(BF16)
    ur[c * NZ + z] = us[z]

    @pl.loop(1, NZ)
    def _(d):
        other = (z + d) % NZ
        send(us.at[other], ur.at[c * NZ + z], snd.at[17], rcv.at[14], (other * NY + y, h))
        send(us.at[other], ur.at[c * NZ + z], snd.at[17], rcv.at[14], (other * NY + y, x * NC + 1 - c))

    send(us.at[z], ur.at[c * NZ + z], snd.at[17], rcv.at[14], partner)
    settle(hid.at[0], rcv.at[5])
    settle(ur.at[pl.ds(0, 15)], rcv.at[14])
    for t in range(2):
        result = hid[t] + jnp.sum(ur[t * NZ : (t + 1) * NZ].astype(F32), axis=0)
        out[t] = jnp.where(c == 0, result[:, :64], result[:, 64:]).astype(BF16)

    for like, n in (
        (qall.at[pl.ds(0, NS - 1)], 0),
        (ps.at[pl.ds(0, NS - 1)], 1),
        (ag.at[pl.ds(0, NS - 1)], 2),
        (hp.at[pl.ds(0, NH - 1)], 3),
        (zb.at[pl.ds(0, NZ - 1)], 4),
        (hid.at[0], 5),
        (x1.at[pl.ds(0, 3)], 6),
        (y2.at[pl.ds(0, 3)], 7),
        (y1.at[pl.ds(0, 3)], 8),
        (x2.at[pl.ds(0, 3)], 9),
        (y1, 10),
        (x2, 11),
        (sb, 12),
        (s1, 13),
        (s2.at[pl.ds(0, 3)], 14),
        (rt1, 15),
        (rt2, 16),
        (ur.at[pl.ds(0, 15)], 17),
    ):
        settle(like, snd.at[n])


def shards(
    lengths,
    block_table,
    slot_request,
    kv_pool,
    new_kv,
    queries,
    residual,
    norm_gain,
    w_out,
    w_gate,
    w_up,
    w_down,
):
    vmem = pl.BlockSpec(memory_space=pltpu.VMEM)
    smem = pl.BlockSpec(memory_space=pltpu.SMEM)
    anywhere = pl.BlockSpec(memory_space=pl.ANY)
    scratch = [
        ((TOKENS, 256), BF16),
        ((TOKENS, HD), BF16),
        ((1024, 512), BF16),
        ((104, 16384), BF16),
        ((104, 16384), BF16),
        ((104, 16384), BF16),
        ((NS, ROWS, HD), BF16),
        ((NS * ROWS, HD), BF16),
        ((PAGE, HD), F32),
        ((NS * ROWS, TOKENS), F32),
        ((NS * ROWS, HD), F32),
        ((NS * ROWS, 256), F32),
        ((NS, 32, HD), BF16),
        ((NS, 32, HD), BF16),
        ((NS, ROWS, HD), BF16),
        ((NS * ROWS, HD), F32),
        ((NH, 32, HD), F32),
        ((NH, 32, HD), F32),
        ((2, 32, HD), F32),
        ((NZ, 48, HD), BF16),
        ((NX, 144, HD), BF16),
        ((NY, 128, HD), BF16),
        ((NY, 528, HD), BF16),
        ((NX, 512, HD), BF16),
        ((NY, 528, HD), BF16),
        ((NX, 512, HD), BF16),
        ((4, 512, HD), F32),
        ((4, 512, HD), F32),
        ((4, 1024, HD), BF16),
        ((4, 1024, HD), BF16),
        ((3, 512, HD), BF16),
        ((3, 512, HD), BF16),
        ((4, 512, HD), BF16),
        ((3, 512, HD), BF16),
        ((4, 128, HD), F32),
        ((4, 128, HD), BF16),
        ((3, 128, HD), BF16),
        ((128, HD), F32),
        ((3, 128, HD), BF16),
        ((3, 128, HD), BF16),
        ((NZ, 32, HD), BF16),
        ((2 * NZ, 32, HD), BF16),
    ]
    return pl.pallas_call(
        kernel,
        out_shape=jax.ShapeDtypeStruct((2, NS, 64), BF16),
        in_specs=[smem, smem] + [vmem] * 5 + [anywhere] * 5,
        out_specs=vmem,
        scratch_shapes=[pltpu.VMEM(shape, kind) for shape, kind in scratch]
        + [pltpu.SemaphoreType.DMA((n,)) for n in (5, 18, 15, 3, 3, 4)],
        compiler_params=pltpu.CompilerParams(
            collective_id=0, has_side_effects=True, vmem_limit_bytes=56 * 1024 * 1024
        ),
    )(
        lengths,
        slot_request,
        block_table,
        new_kv.reshape(3, 256),
        queries.reshape(2, 1024),
        residual,
        norm_gain.reshape(1, 512),
        kv_pool.reshape(TOKENS, 256),
        w_out.reshape(1024, 512),
        w_gate,
        w_up,
        w_down,
    )


def solution(mesh):
    in_specs = (
        P(),
        P(),
        P(),
        P("seq", None, "head", None),
        P(None, "seq", "head", None),
        P(None, "seq", "head", None),
        P(None, None, "seq"),
        P("seq"),
        P("head", None, "seq"),
        P(("seq", "head"), None),
        P(("seq", "head"), None),
        P(("seq", "head"), None),
    )
    out_specs = P(None, None, ("seq", "head"))
    return jax.shard_map(shards, mesh=mesh, in_specs=in_specs, out_specs=out_specs, check_vma=False)
```

```python
import functools
import math

import jax
import jax.numpy as jnp
from jax import lax
from jax.experimental import pallas as pl
from jax.experimental.pallas import tpu as pltpu
from jax.sharding import PartitionSpec as P

EPSILON = 1e-05
NZ, NY, NX, NC = 8, 4, 4, 2
NS, NH = NZ * NY, NX * NC
HD = 128
PAGE = 64
ROWS = 16
TOKENS = 4096
CHUNK = 512
FAR = 131072.0
F32, BF16 = jnp.float32, jnp.bfloat16
NT = (((1,), (1,)), ((), ()))
EXP_SCALE = math.log2(math.e) / math.sqrt(HD)


RING = (1, 3, 2)
AROUND = sorted(
    ((dz, dy) for dz in range(NZ) for dy in range(NY) if dz or dy),
    key=lambda d: -(min(d[0], NZ - d[0]) + min(d[1], NY - d[1])),
)


def iota(shape, dim):
    return lax.broadcasted_iota(jnp.int32, shape, dim)


def kernel(
    lengths, slot_request, table, new_kv, queries, residual, gain,
    kv_hbm, wo_hbm, wg_hbm, wu_hbm, wd_hbm,
    out,
    kv, bias, wo, wg, wu, wd,
    qall, hot, codes, scores, peak, acc,
    ps, pr, ss, sr, ag, af, hp, hr, hid,
    zb, sqz, sqx, sqy, sqp, ga, gb, pa, pb,
    o1, sb, rb, s1, r1, t1, s2, r2, us, ur,
    load_sem, snd, rcv, a2, b2, a3, b3, pa_sem, pb_sem, rb_sem, r1_sem,
):
    s = lax.axis_index("seq")
    h = lax.axis_index("head")
    z, y = s // NY, s % NY
    x, c = h // NC, h % NC
    partner = (s, x * NC + 1 - c)

    def shard(dz, dy):
        return ((z + dz) % NZ) * NY + (y + dy) % NY

    def at_y(other):
        return (z * NY + other, h)

    def at_x(other):
        return (s, other * NC + c)

    def send(src, dst, send_sem, recv_sem, device):
        pltpu.make_async_remote_copy(
            src_ref=src,
            dst_ref=dst,
            send_sem=send_sem,
            recv_sem=recv_sem,
            device_id=device,
            device_id_type=pl.DeviceIdType.MESH,
        ).start()

    def settle(like, sem):
        pltpu.make_async_copy(like, like, sem).wait()

    loads = [
        pltpu.make_async_copy(src, dst, load_sem.at[n])
        for n, (src, dst) in enumerate(
            ((kv_hbm, kv), (wo_hbm, wo), (wg_hbm, wg), (wu_hbm, wu), (wd_hbm, wd))
        )
    ]
    for load in loads:
        load.start()

    barrier = pltpu.get_barrier_semaphore()

    def greet(device):
        pl.semaphore_signal(barrier, inc=1, device_id=device, device_id_type=pl.DeviceIdType.MESH)

    for dz, dy in AROUND:
        greet((shard(dz, dy), h))

    @pl.loop(1, NH)
    def _(d):
        greet((s, (h + d) % NH))

    @pl.loop(1, NZ)
    def _(d):
        greet((((z + d) % NZ) * NY + y, x * NC + 1 - c))

    wide = queries[...].astype(F32)
    own_query = jnp.concatenate(
        [wide[t : t + 1, g * HD : (g + 1) * HD] for t in range(2) for g in range(8)], axis=0
    )
    qall[s] = own_query.astype(BF16)

    pl.semaphore_wait(barrier, (NS - 1) + (NH - 1) + (NZ - 1))

    for dz, dy in AROUND:
        send(qall.at[s], qall.at[s], snd.at[0], rcv.at[0], (shard(dz, dy), h))

    row = iota((NS, HD), 0)
    length = jnp.zeros((NS, HD), jnp.int32)
    slot = jnp.zeros((NS, HD), jnp.int32)
    for r in range(NS):
        length = jnp.where(row == r, lengths[r], length)
        slot = jnp.where(row == slot_request[r], r, slot)
    halves = []
    for half in range(2):
        page = iota((NS, HD), 1) + half * HD
        filled = jnp.clip(length - page * PAGE, 0, PAGE)
        local = jnp.where(filled > 0, table[:, half * HD : (half + 1) * HD] - s * PAGE, -1)
        halves.append((local, (slot * HD + filled).astype(F32)))

    def find(p, carry):
        hits = [jnp.where(local == p, code, 0.0) for local, code in halves]
        codes[pl.ds(p, 1), :] = jnp.sum(hits[0] + hits[1], axis=0, keepdims=True)
        return carry

    lax.fori_loop(0, PAGE, find, 0)
    code = jnp.sum(codes[...], axis=1, keepdims=True)
    codes[...] = jnp.broadcast_to(code, (PAGE, HD))

    def cover(p, carry):
        both = codes[pl.ds(p, 1), :].astype(jnp.int32)
        mine = (iota((PAGE, HD), 1) == both // HD) & (iota((PAGE, HD), 0) < both % HD)
        bias[pl.ds(pl.multiple_of(p * PAGE, PAGE), PAGE), :] = jnp.where(mine, 0.0, -FAR).astype(BF16)
        return carry

    lax.fori_loop(0, PAGE, cover, 0)
    hot[...] = jnp.where(iota((NS * ROWS, HD), 0) // ROWS == iota((NS * ROWS, HD), 1), 1.0, 0.0).astype(BF16)

    loads[0].wait()
    settle(qall.at[pl.ds(0, NS - 1)], rcv.at[0])

    aug_query = jnp.concatenate([qall[...].reshape(NS * ROWS, HD), hot[...]], axis=1)
    peak[...] = jnp.full((NS * ROWS, HD), -4.0 * FAR, F32)

    def score(k, carry):
        tokens = pl.ds(pl.multiple_of(k * CHUNK, CHUNK), CHUNK)
        aug_key = jnp.concatenate([kv[tokens, :HD], bias[tokens, :]], axis=1)
        raw = lax.dot_general(aug_query, aug_key, NT, preferred_element_type=F32)
        scores[:, tokens] = raw
        peak[...] = jnp.maximum(peak[...], functools.reduce(jnp.maximum, [raw[:, n : n + HD] for n in range(0, CHUNK, HD)]))
        return carry

    lax.fori_loop(0, TOKENS // CHUNK, score, 0, unroll=True)
    top = jnp.max(peak[...], axis=1, keepdims=True).astype(BF16).astype(F32)
    peak[...] = jnp.broadcast_to(top, (NS * ROWS, HD))
    acc[...] = jnp.zeros((NS * ROWS, 2 * HD), F32)

    def mix(k, carry):
        tokens = pl.ds(pl.multiple_of(k * CHUNK, CHUNK), CHUNK)
        aug_value = jnp.concatenate([kv[tokens, HD:], jnp.ones((CHUNK, HD), BF16)], axis=1)
        base = jnp.concatenate([peak[...]] * (CHUNK // HD), axis=1)
        weights = jnp.exp2((scores[:, tokens] - base) * EXP_SCALE).astype(BF16)
        acc[...] += jnp.dot(weights, aug_value, preferred_element_type=F32)
        return carry

    lax.fori_loop(0, TOKENS // CHUNK, mix, 0, unroll=True)
    acc_rows = acc[:, :HD].astype(BF16).reshape(NS, ROWS, HD)
    ps[...] = acc_rows
    cube = (NS, ROWS, HD)
    lane, line = iota(cube, 2), iota(cube, 1)
    stats = jnp.where(lane == line, peak[...].reshape(cube), 0.0)
    stats = jnp.where(lane == line + ROWS, acc[:, HD:].reshape(cube), stats)
    ss[...] = jnp.sum(stats, axis=1, keepdims=True)
    pr[s] = ps[s]
    sr[s] = ss[s]
    for dz, dy in AROUND:
        other = shard(dz, dy)
        send(ps.at[other], pr.at[s], snd.at[1], rcv.at[1], (other, h))
        send(ss.at[other], sr.at[s], snd.at[20], rcv.at[13], (other, h))

    fresh = new_kv[...].astype(F32)
    late = iota((ROWS, 1), 0) >= ROWS // 2
    rounded_query = own_query.astype(BF16).astype(F32)
    fresh_scores = []
    for e in range(3):
        raw = jnp.sum(rounded_query * fresh[e : e + 1, :HD], axis=1, keepdims=True)
        fresh_scores.append(jnp.where(late, raw, -FAR) if e == 2 else raw)
    settle(pr.at[pl.ds(0, NS - 1)], rcv.at[1])
    settle(sr.at[pl.ds(0, NS - 1)], rcv.at[13])
    stats = jnp.broadcast_to(sr[...], cube)
    tops = jnp.sum(jnp.where(lane == line, stats, 0.0), axis=2, keepdims=True)
    sums = jnp.sum(jnp.where(lane == line + ROWS, stats, 0.0), axis=2, keepdims=True)
    top = jnp.max(tops, axis=0)
    for raw in fresh_scores:
        top = jnp.maximum(top, raw)
    factor = jnp.exp2((tops - top[None]) * EXP_SCALE)
    total = jnp.sum(factor * sums, axis=0)
    mixed = jnp.sum(factor * pr[...].astype(F32), axis=0)
    for e, raw in enumerate(fresh_scores):
        weight = jnp.exp2((raw - top) * EXP_SCALE).astype(BF16).astype(F32)
        total = total + weight
        mixed = mixed + weight * fresh[e : e + 1, HD:]
    ag[s] = (mixed / total).astype(BF16)

    for dz, dy in AROUND:
        send(ag.at[s], ag.at[s], snd.at[2], rcv.at[2], (shard(dz, dy), h))

    loads[1].wait()
    settle(ag.at[pl.ds(0, NS - 1)], rcv.at[2])

    af[...] = ag[...].reshape(NS * ROWS, HD).astype(F32)
    attended = jnp.concatenate(
        [
            jnp.concatenate([af[pl.ds(t * 8 + g, NS, stride=ROWS), :] for g in range(8)], axis=1)
            for t in range(2)
        ],
        axis=0,
    ).astype(BF16)
    part = jnp.dot(attended, wo[...], preferred_element_type=F32)
    for xx in range(NX):
        for cc in range(NC):
            hp[xx * NC + cc] = part[cc * NS : (cc + 1) * NS, xx * HD : (xx + 1) * HD]
    hr[h] = hp[h]

    @pl.loop(1, NH)
    def _(d):
        other = (h + d) % NH
        send(hp.at[other], hr.at[h], snd.at[3], rcv.at[3], (s, other))

    columns = pl.ds(pl.multiple_of(x * HD, HD), HD)
    settle(hr.at[pl.ds(0, NH - 1)], rcv.at[3])
    hidden = residual[c, :, columns].astype(F32) + jnp.sum(hr[...], axis=0)
    hid[c] = hidden
    square = jnp.sum(hidden * hidden, axis=1, keepdims=True)
    zb[z] = (hidden * gain[:, columns]).astype(BF16)
    spread = jnp.where(iota((NS, HD), 0) == iota((NS, HD), 1), square, 0.0)
    sqz[z] = jnp.sum(spread, axis=0, keepdims=True)

    for d in (4, 3, 5, 2, 6, 1, 7):
        there = (((z + d) % NZ) * NY + y, h)
        send(zb.at[z], zb.at[z], snd.at[4], rcv.at[4], there)
        send(sqz.at[z], sqz.at[z], snd.at[5], rcv.at[5], there)
    send(hid.at[c], hid.at[c], snd.at[6], rcv.at[6], partner)
    settle(zb.at[pl.ds(0, NZ - 1)], rcv.at[4])

    ga[y, x] = zb[0:4].reshape(128, HD)
    gb[x, y] = zb[4:8].reshape(128, HD)

    def on_a(xx, n):
        for d in RING:
            send(ga.at[y, xx], ga.at[y, xx], snd.at[9], a3.at[n, d - 1], at_y((y + d) % NY))

    def on_b(yy, n):
        for d in RING:
            send(gb.at[x, yy], gb.at[x, yy], snd.at[10], b3.at[n, d - 1], at_x((x + d) % NX))

    def across(yy, xx, n):
        send(ga.at[yy, xx], pa.at[yy, xx], snd.at[11], pa_sem.at[n], partner)

    def across_b(xx, yy, n):
        send(gb.at[xx, yy], pb.at[xx, yy], snd.at[12], pb_sem.at[n], partner)

    for d in RING:
        send(ga.at[y, x], ga.at[y, x], snd.at[7], a2.at[d - 1], at_x((x + d) % NX))
        send(gb.at[x, y], gb.at[x, y], snd.at[8], b2.at[d - 1], at_y((y + d) % NY))
    on_a(x, 0)
    on_b(y, 0)
    across(y, x, 0)
    across_b(x, y, 0)
    settle(sqz.at[pl.ds(0, NZ - 1)], rcv.at[5])
    sqx[x] = jnp.sum(sqz[...], axis=0)
    for d in RING:
        send(sqx.at[x], sqx.at[x], snd.at[13], rcv.at[7], at_x((x + d) % NX))

    done = []
    done.append(("a", y, x, 0))
    done.append(("b", x, y, 0))
    for n, d in enumerate(RING):
        xx, yy = (x + NX - d) % NX, (y + NY - d) % NY
        settle(ga.at[y, xx], a2.at[d - 1])
        on_a(xx, n + 1)
        across(y, xx, n + 1)
        done.append(("a", y, xx, n + 1))
        settle(gb.at[x, yy], b2.at[d - 1])
        on_b(yy, n + 1)
        across_b(x, yy, n + 1)
        done.append(("b", x, yy, n + 1))
    settle(sqx.at[pl.ds(0, NX - 1)], rcv.at[7])
    sqy[y] = jnp.sum(sqx[...], axis=0)
    for d in RING:
        send(sqy.at[y], sqy.at[y], snd.at[14], rcv.at[8], at_y((y + d) % NY))

    loads[2].wait()
    loads[3].wait()
    gate = jnp.zeros((64, 104), F32)
    up = jnp.zeros((64, 104), F32)

    def multiply(item, sums):
        half, outer, inner, n = item
        if half == "a":
            settle(pa.at[outer, inner], pa_sem.at[n])
            own, other, yy, xx, first = ga, pa, outer, inner, 0
        else:
            settle(pb.at[outer, inner], pb_sem.at[n])
            own, other, yy, xx, first = gb, pb, inner, outer, 4
        stream = jnp.concatenate(
            [
                jnp.concatenate([ref[outer, inner, zz * 32 : (zz + 1) * 32] for zz in range(4)], axis=1)
                for ref in (own, other)
            ],
            axis=0,
        )
        where = [
            pl.ds(pl.multiple_of((first + zz) * 2048 + yy * 512 + xx * HD, HD), HD) for zz in range(4)
        ]
        return tuple(
            total
            + lax.dot_general(
                stream,
                jnp.concatenate([ref[:, w] for w in where], axis=1),
                NT,
                preferred_element_type=F32,
            )
            for total, ref in zip(sums, (wg, wu), strict=True)
        )

    sums = (gate, up)
    arrivals = []
    for n, k in enumerate((0,) + RING):
        for d in RING:
            arrivals.append(("a", (y + NY - d) % NY, (x + NX - k) % NX, n, d))
            arrivals.append(("b", (x + NX - d) % NX, (y + NY - k) % NY, n, d))
    for m, (half, outer, inner, n, d) in enumerate(arrivals):
        place = 4 + m // 2
        if half == "a":
            settle(ga.at[outer, inner], a3.at[n, d - 1])
            across(outer, inner, place)
        else:
            settle(gb.at[outer, inner], b3.at[n, d - 1])
            across_b(outer, inner, place)
        done.append((half, outer, inner, place))
        for _ in range(1 if m < len(arrivals) - 8 else 1):
            sums = multiply(done.pop(0), sums)
    for item in done:
        sums = multiply(item, sums)
    gate, up = sums
    settle(sqy.at[pl.ds(0, NY - 1)], rcv.at[8])
    sqp[0] = jnp.sum(sqy[...], axis=0)
    send(sqp.at[0], sqp.at[1], snd.at[15], rcv.at[9], partner)
    settle(sqp.at[0], rcv.at[9])
    square = jnp.concatenate(
        [
            jnp.sum(
                jnp.where(iota((NS, HD), 0) == iota((NS, HD), 1), sqp[n], 0.0), axis=1, keepdims=True
            )
            for n in range(2)
        ],
        axis=0,
    )
    scale = lax.rsqrt(square * (1.0 / 16384.0) + EPSILON)
    gate = gate * scale
    up = up * scale
    activation = (gate / (1.0 + jnp.exp(-gate)) * up).astype(BF16)

    loads[4].wait()
    turn = RING + (0,)
    spots = [[(y + b) % NY, (x + b) % NX] for b in turn]

    def groups(k):
        return [(spots[b][0], spots[k][1], 0) for b in range(4)] + [
            (spots[k][0], spots[b][1], 4) for b in range(4)
        ]

    def down(k):
        for m, (yy, xx, first) in enumerate(groups(k)):
            weight = jnp.concatenate(
                [
                    wd[:, pl.ds(pl.multiple_of((first + zz) * 2048 + yy * 512 + xx * HD, HD), HD)]
                    for zz in range(4)
                ],
                axis=1,
            )
            block = jnp.dot(activation, weight, preferred_element_type=F32)
            for zz in range(4):
                at = slice(m * 128 + zz * 32, m * 128 + (zz + 1) * 32)
                piece = block[:, zz * HD : (zz + 1) * HD]
                o1[k, at] = piece[0:32]
                sb[k, at] = piece[32:64].astype(BF16)
        send(sb.at[k], rb.at[k], snd.at[16], rb_sem.at[k], partner)

    def finish(k):
        settle(rb.at[k], rb_sem.at[k])
        for half in range(2):
            for b in range(4):
                at = slice((half * 4 + b) * 128, (half * 4 + b + 1) * 128)
                whole = o1[k, at] + rb[k, at].astype(F32)
                if b == 3:
                    t1[k, half] = whole
                else:
                    s1[k, half * 3 + b] = whole.astype(BF16)
                    there = at_x(spots[b][1]) if half else at_y(spots[b][0])
                    send(s1.at[k, half * 3 + b], r1.at[k, half * 3 + b], snd.at[17], r1_sem.at[k], there)

    def reduce_one(k):
        settle(r1.at[k], r1_sem.at[k])
        for half in range(2):
            whole = t1[k, half]
            for b in range(3):
                whole = whole + r1[k, half * 3 + b].astype(F32)
            if k == 3:
                t1[k, half] = whole
            else:
                s2[half, k] = whole.astype(BF16)
                there = at_y(spots[k][0]) if half else at_x(spots[k][1])
                send(s2.at[half, k], r2.at[half, k], snd.at[18], rcv.at[10 + half], there)

    for k in range(4):
        down(k)
        if k > 0:
            finish(k - 1)
    finish(3)
    for k in range(4):
        reduce_one(k)
    for half in range(2):
        settle(r2.at[half], rcv.at[10 + half])
        whole = t1[3, half]
        for b in range(3):
            whole = whole + r2[half, b].astype(F32)
        us[half * 4 : half * 4 + 4] = whole.reshape(4, 32, HD).astype(BF16)
    ur[c * NZ + z] = us[z]
    for d in (4, 3, 5, 2, 6, 1, 7):
        other = (z + d) % NZ
        send(us.at[other], ur.at[c * NZ + z], snd.at[19], rcv.at[12], (other * NY + y, h))
        send(us.at[other], ur.at[c * NZ + z], snd.at[19], rcv.at[12], (other * NY + y, x * NC + 1 - c))
    send(us.at[z], ur.at[c * NZ + z], snd.at[19], rcv.at[12], partner)
    settle(hid.at[0], rcv.at[6])
    settle(ur.at[pl.ds(0, 15)], rcv.at[12])
    for t in range(2):
        result = hid[t] + jnp.sum(ur[t * NZ : (t + 1) * NZ].astype(F32), axis=0)
        out[t] = jnp.where(c == 0, result[:, :64], result[:, 64:]).astype(BF16)

    for like, n in (
        (qall.at[pl.ds(0, NS - 1)], 0),
        (ps.at[pl.ds(0, NS - 1)], 1),
        (ss.at[pl.ds(0, NS - 1)], 20),
        (ag.at[pl.ds(0, NS - 1)], 2),
        (hp.at[pl.ds(0, NH - 1)], 3),
        (zb.at[pl.ds(0, NZ - 1)], 4),
        (sqz.at[pl.ds(0, NZ - 1)], 5),
        (hid.at[0], 6),
        (s2.at[0], 7),
        (s2.at[0], 8),
        (ga.at[pl.ds(0, 3)], 9),
        (gb.at[pl.ds(0, 3)], 10),
        (ga, 11),
        (gb, 12),
        (sqx.at[pl.ds(0, NX - 1)], 13),
        (sqy.at[pl.ds(0, NY - 1)], 14),
        (sqp.at[0], 15),
        (sb, 16),
        (s1, 17),
        (s2, 18),
        (ur.at[pl.ds(0, 15)], 19),
    ):
        settle(like, snd.at[n])


def shards(
    lengths,
    block_table,
    slot_request,
    kv_pool,
    new_kv,
    queries,
    residual,
    norm_gain,
    w_out,
    w_gate,
    w_up,
    w_down,
):
    vmem = pl.BlockSpec(memory_space=pltpu.VMEM)
    smem = pl.BlockSpec(memory_space=pltpu.SMEM)
    anywhere = pl.BlockSpec(memory_space=pl.ANY)
    scratch = [
        ((TOKENS, 256), BF16),
        ((TOKENS, HD), BF16),
        ((1024, 512), BF16),
        ((104, 16384), BF16),
        ((104, 16384), BF16),
        ((104, 16384), BF16),
        ((NS, ROWS, HD), BF16),
        ((NS * ROWS, HD), BF16),
        ((PAGE, HD), F32),
        ((NS * ROWS, TOKENS), F32),
        ((NS * ROWS, HD), F32),
        ((NS * ROWS, 256), F32),
        ((NS, ROWS, HD), BF16),
        ((NS, ROWS, HD), BF16),
        ((NS, 1, HD), F32),
        ((NS, 1, HD), F32),
        ((NS, ROWS, HD), BF16),
        ((NS * ROWS, HD), F32),
        ((NH, 32, HD), F32),
        ((NH, 32, HD), F32),
        ((2, 32, HD), F32),
        ((NZ, 32, HD), BF16),
        ((NZ, 1, HD), F32),
        ((NX, 1, HD), F32),
        ((NY, 1, HD), F32),
        ((2, 1, HD), F32),
        ((NY, NX, 128, HD), BF16),
        ((NX, NY, 128, HD), BF16),
        ((NY, NX, 128, HD), BF16),
        ((NX, NY, 128, HD), BF16),
        ((4, 1024, HD), F32),
        ((4, 1024, HD), BF16),
        ((4, 1024, HD), BF16),
        ((4, 6, 128, HD), BF16),
        ((4, 6, 128, HD), BF16),
        ((4, 2, 128, HD), F32),
        ((2, 3, 128, HD), BF16),
        ((2, 3, 128, HD), BF16),
        ((NZ, 32, HD), BF16),
        ((2 * NZ, 32, HD), BF16),
    ]
    return pl.pallas_call(
        kernel,
        out_shape=jax.ShapeDtypeStruct((2, NS, 64), BF16),
        in_specs=[smem, smem] + [vmem] * 5 + [anywhere] * 5,
        out_specs=vmem,
        scratch_shapes=[pltpu.VMEM(shape, kind) for shape, kind in scratch]
        + [
            pltpu.SemaphoreType.DMA(n)
            for n in ((5,), (21,), (14,), (3,), (3,), (4, 3), (4, 3), (16,), (16,), (4,), (4,))
        ],
        compiler_params=pltpu.CompilerParams(
            collective_id=0, has_side_effects=True, vmem_limit_bytes=56 * 1024 * 1024
        ),
    )(
        lengths,
        slot_request,
        block_table,
        new_kv.reshape(3, 256),
        queries.reshape(2, 1024),
        residual,
        norm_gain.reshape(1, 512),
        kv_pool.reshape(TOKENS, 256),
        w_out.reshape(1024, 512),
        w_gate,
        w_up,
        w_down,
    )


def solution(mesh):
    in_specs = (
        P(),
        P(),
        P(),
        P("seq", None, "head", None),
        P(None, "seq", "head", None),
        P(None, "seq", "head", None),
        P(None, None, "seq"),
        P("seq"),
        P("head", None, "seq"),
        P(("seq", "head"), None),
        P(("seq", "head"), None),
        P(("seq", "head"), None),
    )
    out_specs = P(None, None, ("seq", "head"))
    return jax.shard_map(shards, mesh=mesh, in_specs=in_specs, out_specs=out_specs, check_vma=False)
```

```python
import functools
import math

import jax
import jax.numpy as jnp
from jax import lax
from jax.experimental import pallas as pl
from jax.experimental.pallas import tpu as pltpu
from jax.sharding import PartitionSpec as P

EPSILON = 1e-05
NZ, NY, NX, NC = 8, 4, 4, 2
NS, NH = NZ * NY, NX * NC
HD = 128
PAGE = 64
ROWS = 16
TOKENS = 4096
CHUNK = 512
APART = (0, 1, 2, 3, 7, 6, 5, 4)
LAG = 12
BATCH, LAST_BATCH = 12, 8
FAR = 131072.0
F32, BF16 = jnp.float32, jnp.bfloat16
NT = (((1,), (1,)), ((), ()))
EXP_SCALE = math.log2(math.e) / math.sqrt(HD)


RING = (1, 3, 2)
AROUND = sorted(
    ((dz, dy) for dz in range(NZ) for dy in range(NY) if dz or dy),
    key=lambda d: -(min(d[0], NZ - d[0]) + min(d[1], NY - d[1])),
)


def iota(shape, dim):
    return lax.broadcasted_iota(jnp.int32, shape, dim)


def kernel(
    lengths, slot_request, new_kv, queries,
    table_hbm, residual_hbm, gain_hbm, kv_hbm, wo_hbm, wg_hbm, wu_hbm, wd_hbm,
    out,
    table, residual, gain, kv, bias, wo, wg, wu, wd,
    qall, hot, codes, scores, peak, acc,
    ps, pr, ss, sr, ag, af, hp, hr, hid,
    sqz, sqx, sqy, sqp, ga, gb, pa, pb,
    o1, sb, rb, s1, r1, t1, fs, fr,
    load_sem, snd, rcv, z_sem, a2, b2, a3, b3, pa_sem, pb_sem, rb_sem, r1_sem,
):
    s = lax.axis_index("seq")
    h = lax.axis_index("head")
    z, y = s // NY, s % NY
    x, c = h // NC, h % NC
    partner = (s, x * NC + 1 - c)

    def shard(dz, dy):
        return ((z + dz) % NZ) * NY + (y + dy) % NY

    def at_y(other):
        return (z * NY + other, h)

    def at_x(other):
        return (s, other * NC + c)

    def send(src, dst, send_sem, recv_sem, device):
        pltpu.make_async_remote_copy(
            src_ref=src,
            dst_ref=dst,
            send_sem=send_sem,
            recv_sem=recv_sem,
            device_id=device,
            device_id_type=pl.DeviceIdType.MESH,
        ).start()

    def settle(like, sem):
        pltpu.make_async_copy(like, like, sem).wait()

    barrier = pltpu.get_barrier_semaphore()

    def greet(device):
        pl.semaphore_signal(barrier, inc=1, device_id=device, device_id_type=pl.DeviceIdType.MESH)

    for dz, dy in AROUND:
        greet((shard(dz, dy), h))

    @pl.loop(1, NH)
    def _(d):
        greet((s, (h + d) % NH))

    @pl.loop(1, NZ)
    def _(d):
        greet((((z + d) % NZ) * NY + y, x * NC + 1 - c))

    loads = [
        pltpu.make_async_copy(src, dst, load_sem.at[n])
        for n, (src, dst) in enumerate(
            (
                (kv_hbm, kv),
                (wo_hbm, wo),
                (wg_hbm, wg),
                (wu_hbm, wu),
                (wd_hbm, wd),
                (table_hbm, table),
                (residual_hbm, residual),
                (gain_hbm, gain),
            )
        )
    ]
    for n in (5, 0, 1, 6, 7, 2, 3, 4):
        loads[n].start()

    wide = queries[...].astype(F32)
    own_query = jnp.concatenate(
        [wide[t : t + 1, g * HD : (g + 1) * HD] for t in range(2) for g in range(8)], axis=0
    )
    qall[s] = own_query.astype(BF16)

    pl.semaphore_wait(barrier, (NS - 1) + (NH - 1) + (NZ - 1))

    for dz, dy in AROUND:
        send(qall.at[s], qall.at[s], snd.at[0], rcv.at[0], (shard(dz, dy), h))

    loads[5].wait()
    row = iota((NS, HD), 0)
    length = jnp.zeros((NS, HD), jnp.int32)
    slot = jnp.zeros((NS, HD), jnp.int32)
    for r in range(NS):
        length = jnp.where(row == r, lengths[r], length)
        slot = jnp.where(row == slot_request[r], r, slot)
    halves = []
    for half in range(2):
        page = iota((NS, HD), 1) + half * HD
        filled = jnp.clip(length - page * PAGE, 0, PAGE)
        local = jnp.where(filled > 0, table[:, half * HD : (half + 1) * HD] - s * PAGE, -1)
        halves.append((local, (slot * HD + filled).astype(F32)))

    def find(p, carry):
        hits = [jnp.where(local == p, code, 0.0) for local, code in halves]
        codes[pl.ds(p, 1), :] = jnp.sum(hits[0] + hits[1], axis=0, keepdims=True)
        return carry

    lax.fori_loop(0, PAGE, find, 0)
    code = jnp.sum(codes[...], axis=1, keepdims=True)
    codes[...] = jnp.broadcast_to(code, (PAGE, HD))

    def cover(p, carry):
        both = codes[pl.ds(p, 1), :].astype(jnp.int32)
        mine = (iota((PAGE, HD), 1) == both // HD) & (iota((PAGE, HD), 0) < both % HD)
        bias[pl.ds(pl.multiple_of(p * PAGE, PAGE), PAGE), :] = jnp.where(mine, 0.0, -FAR).astype(BF16)
        return carry

    lax.fori_loop(0, PAGE, cover, 0)
    hot[...] = jnp.where(iota((NS * ROWS, HD), 0) // ROWS == iota((NS * ROWS, HD), 1), 1.0, 0.0).astype(BF16)

    loads[0].wait()
    settle(qall.at[pl.ds(0, NS - 1)], rcv.at[0])

    aug_query = jnp.concatenate([qall[...].reshape(NS * ROWS, HD), hot[...]], axis=1)
    peak[...] = jnp.full((NS * ROWS, HD), -4.0 * FAR, F32)

    def score(k, carry):
        tokens = pl.ds(pl.multiple_of(k * CHUNK, CHUNK), CHUNK)
        aug_key = jnp.concatenate([kv[tokens, :HD], bias[tokens, :]], axis=1)
        raw = lax.dot_general(aug_query, aug_key, NT, preferred_element_type=F32)
        scores[:, tokens] = raw
        peak[...] = jnp.maximum(peak[...], functools.reduce(jnp.maximum, [raw[:, n : n + HD] for n in range(0, CHUNK, HD)]))
        return carry

    lax.fori_loop(0, TOKENS // CHUNK, score, 0, unroll=True)
    top = jnp.max(peak[...], axis=1, keepdims=True).astype(BF16).astype(F32)
    peak[...] = jnp.broadcast_to(top, (NS * ROWS, HD))
    acc[...] = jnp.zeros((NS * ROWS, 2 * HD), F32)

    def mix(k, carry):
        tokens = pl.ds(pl.multiple_of(k * CHUNK, CHUNK), CHUNK)
        aug_value = jnp.concatenate([kv[tokens, HD:], jnp.ones((CHUNK, HD), BF16)], axis=1)
        base = jnp.concatenate([peak[...]] * (CHUNK // HD), axis=1)
        weights = jnp.exp2((scores[:, tokens] - base) * EXP_SCALE).astype(BF16)
        acc[...] += jnp.dot(weights, aug_value, preferred_element_type=F32)
        return carry

    lax.fori_loop(0, TOKENS // CHUNK, mix, 0, unroll=True)
    acc_rows = acc[:, :HD].astype(BF16).reshape(NS, ROWS, HD)
    ps[...] = acc_rows
    cube = (NS, ROWS, HD)
    lane, line = iota(cube, 2), iota(cube, 1)
    stats = jnp.where(lane == line, peak[...].reshape(cube), 0.0)
    stats = jnp.where(lane == line + ROWS, acc[:, HD:].reshape(cube), stats)
    ss[...] = jnp.sum(stats, axis=1, keepdims=True)
    pr[s] = ps[s]
    sr[s] = ss[s]
    for dz, dy in AROUND:
        other = shard(dz, dy)
        send(ps.at[other], pr.at[s], snd.at[1], rcv.at[1], (other, h))
        send(ss.at[other], sr.at[s], snd.at[20], rcv.at[13], (other, h))

    fresh = new_kv[...].astype(F32)
    late = iota((ROWS, 1), 0) >= ROWS // 2
    rounded_query = own_query.astype(BF16).astype(F32)
    fresh_scores = []
    for e in range(3):
        raw = jnp.sum(rounded_query * fresh[e : e + 1, :HD], axis=1, keepdims=True)
        fresh_scores.append(jnp.where(late, raw, -FAR) if e == 2 else raw)
    settle(pr.at[pl.ds(0, NS - 1)], rcv.at[1])
    settle(sr.at[pl.ds(0, NS - 1)], rcv.at[13])
    stats = jnp.broadcast_to(sr[...], cube)
    tops = jnp.sum(jnp.where(lane == line, stats, 0.0), axis=2, keepdims=True)
    sums = jnp.sum(jnp.where(lane == line + ROWS, stats, 0.0), axis=2, keepdims=True)
    top = jnp.max(tops, axis=0)
    for raw in fresh_scores:
        top = jnp.maximum(top, raw)
    factor = jnp.exp2((tops - top[None]) * EXP_SCALE)
    total = jnp.sum(factor * sums, axis=0)
    mixed = jnp.sum(factor * pr[...].astype(F32), axis=0)
    for e, raw in enumerate(fresh_scores):
        weight = jnp.exp2((raw - top) * EXP_SCALE).astype(BF16).astype(F32)
        total = total + weight
        mixed = mixed + weight * fresh[e : e + 1, HD:]
    ag[s] = (mixed / total).astype(BF16)

    for dz, dy in AROUND:
        send(ag.at[s], ag.at[s], snd.at[2], rcv.at[2], (shard(dz, dy), h))

    loads[1].wait()
    loads[6].wait()
    loads[7].wait()
    settle(ag.at[pl.ds(0, NS - 1)], rcv.at[2])

    af[...] = ag[...].reshape(NS * ROWS, HD).astype(F32)
    attended = jnp.concatenate(
        [
            jnp.concatenate([af[pl.ds(t * 8 + g, NS, stride=ROWS), :] for g in range(8)], axis=1)
            for t in range(2)
        ],
        axis=0,
    ).astype(BF16)
    part = jnp.dot(attended, wo[...], preferred_element_type=F32)
    for xx in range(NX):
        for cc in range(NC):
            hp[xx * NC + cc] = part[cc * NS : (cc + 1) * NS, xx * HD : (xx + 1) * HD]
    hr[h] = hp[h]

    @pl.loop(1, NH)
    def _(d):
        other = (h + d) % NH
        send(hp.at[other], hr.at[h], snd.at[3], rcv.at[3], (s, other))

    columns = pl.ds(pl.multiple_of(x * HD, HD), HD)
    settle(hr.at[pl.ds(0, NH - 1)], rcv.at[3])
    hidden = residual[c, :, columns].astype(F32) + jnp.sum(hr[...], axis=0)
    hid[c] = hidden
    square = jnp.sum(hidden * hidden, axis=1, keepdims=True)
    halves = ((ga, pa, a2, a3, pa_sem, x, y, at_x, at_y), (gb, pb, b2, b3, pb_sem, y, x, at_y, at_x))
    ga[y, x, 0:32] = (hidden * gain[:, columns]).astype(BF16)
    spread = jnp.where(iota((NS, HD), 0) == iota((NS, HD), 1), square, 0.0)
    sqz[z] = jnp.sum(spread, axis=0, keepdims=True)
    own = ga.at[y, x, pl.ds(0, 32)]
    for p in range(1, NZ):
        there = (((z + NZ - APART[p]) % NZ) * NY + y, h)
        place = ga.at[y, x, pl.ds(p * 32, 32)] if p < 4 else gb.at[x, y, pl.ds((p - 4) * 32, 32)]
        send(own, place, snd.at[4], z_sem.at[p // 2], there)
    for d in (4, 3, 5, 2, 6, 1, 7):
        there = (((z + d) % NZ) * NY + y, h)
        send(sqz.at[z], sqz.at[z], snd.at[5], rcv.at[5], there)
    send(hid.at[c], hid.at[c], snd.at[6], rcv.at[6], partner)
    done = []

    def block(ref, outer, inner, w):
        return ref.at[outer, inner, pl.ds(w * 64, 64)]

    def pass_on(half, w, inner, n):
        full, _, _, last, _, _, outer, _, at_last = halves[half]
        here = block(full, outer, inner, w)
        for d in RING:
            send(here, here, snd.at[9 + half], last.at[w, n, d - 1], at_last((outer + d) % 4))
        cross(half, w, outer, inner, n)

    def cross(half, w, outer, inner, n):
        full, other, _, _, sem, _, _, _, _ = halves[half]
        send(block(full, outer, inner, w), block(other, outer, inner, w), snd.at[11 + half], sem.at[w, n], partner)
        done.append((half, w, outer, inner, n))

    for w in range(2):
        for half in range(2):
            full, _, first, _, _, inner, outer, at_first, _ = halves[half]
            here = block(full, outer, inner, w)
            if half == 0 and w == 0:
                settle(own, z_sem.at[0])
            else:
                settle(here, z_sem.at[half * 2 + w])
            for d in RING:
                send(here, here, snd.at[7 + half], first.at[w, d - 1], at_first((inner + d) % 4))
            pass_on(half, w, inner, 0)
    settle(sqz.at[pl.ds(0, NZ - 1)], rcv.at[5])
    sqx[x] = jnp.sum(sqz[...], axis=0)
    for d in RING:
        send(sqx.at[x], sqx.at[x], snd.at[13], rcv.at[7], at_x((x + d) % NX))

    loads[2].wait()
    loads[3].wait()

    def multiply(items, sums):
        for half, w, outer, inner, n in items:
            full, other, _, _, sem, _, _, _, _ = halves[half]
            settle(block(other, outer, inner, w), sem.at[w, n])
        gate, up = sums
        for half, w, outer, inner, n in items:
            full, other, _, _, _, _, _, _, _ = halves[half]
            yy, xx = (inner, outer) if half else (outer, inner)
            both = (2 * w, 2 * w + 1)
            stream = jnp.concatenate(
                [
                    jnp.concatenate([ref[outer, inner, p * 32 : (p + 1) * 32] for p in both], axis=1)
                    for ref in (full, other)
                ],
                axis=0,
            )
            zs = [(z + APART[half * 4 + p]) % NZ for p in both]
            where = [pl.ds(pl.multiple_of(zz * 2048 + yy * 512 + xx * HD, HD), HD) for zz in zs]
            left = [jnp.concatenate([ref[:, at] for at in where], axis=1) for ref in (wg, wu)]
            gate = gate + lax.dot_general(left[0], stream, NT, preferred_element_type=F32)
            up = up + lax.dot_general(left[1], stream, NT, preferred_element_type=F32)
        return gate, up

    def catch_up(lag, batch, sums):
        while len(done) >= lag + batch:
            sums = multiply([done.pop(0) for _ in range(batch)], sums)
        return sums

    sums = (jnp.zeros((104, 64), F32), jnp.zeros((104, 64), F32))

    def last_arrivals(w, half, n, k):
        full, _, _, last, _, inner, outer, _, _ = halves[half]
        for d in RING:
            there, beside = (outer + 4 - d) % 4, (inner + 4 - k) % 4
            settle(block(full, there, beside, w), last.at[w, n, d - 1])
            cross(half, w, there, beside, 3 * n + 3 + d)

    for w in range(2):
        for half in range(2):
            full, _, first, _, _, inner, outer, _, _ = halves[half]
            for n, d in enumerate(RING):
                beside = (inner + 4 - d) % 4
                settle(block(full, outer, beside, w), first.at[w, d - 1])
                pass_on(half, w, beside, n + 1)
        for half in range(2):
            last_arrivals(w, half, 0, 0)
    settle(sqx.at[pl.ds(0, NX - 1)], rcv.at[7])
    sqy[y] = jnp.sum(sqx[...], axis=0)
    for d in RING:
        send(sqy.at[y], sqy.at[y], snd.at[14], rcv.at[8], at_y((y + d) % NY))
    sums = catch_up(LAG, BATCH, sums)
    for w in range(2):
        for n, k in enumerate(RING):
            for half in range(2):
                last_arrivals(w, half, n + 1, k)
                sums = catch_up(LAG, BATCH, sums)
        if w == 0:
            settle(sqy.at[pl.ds(0, NY - 1)], rcv.at[8])
            sqp[0] = jnp.sum(sqy[...], axis=0)
            send(sqp.at[0], sqp.at[1], snd.at[15], rcv.at[9], partner)
    sums = catch_up(LAST_BATCH, BATCH, sums)
    while done:
        sums = catch_up(0, min(LAST_BATCH, len(done)), sums)
    settle(sqp.at[0], rcv.at[9])
    square = jnp.broadcast_to(sqp[0], (8, HD)) + pltpu.roll(jnp.broadcast_to(sqp[1], (8, HD)), 32, 1)
    scale = lax.rsqrt(square[0:1, 0:64] * (1.0 / 16384.0) + EPSILON)
    gate = sums[0] * scale
    up = sums[1] * scale
    activation = (gate / (1.0 + jnp.exp(-gate)) * up).T.astype(BF16)

    loads[4].wait()
    turn = (2, 1, 3, 0)
    spots = [[(y + b) % NY, (x + b) % NX] for b in turn]

    def groups(r):
        k, first = r % 4, r // 4 * 4
        return [(spots[b][0], spots[k][1], first) for b in range(4)] + [
            (spots[k][0], spots[b][1], first + 2) for b in range(4)
        ]

    def down(r):
        for m, (yy, xx, first) in enumerate(groups(r)):
            weight = jnp.concatenate(
                [
                    wd[:, pl.ds(pl.multiple_of((first + zz) * 2048 + yy * 512 + xx * HD, HD), HD)]
                    for zz in range(2)
                ],
                axis=1,
            )
            product = jnp.dot(activation, weight, preferred_element_type=F32)
            for zz in range(2):
                at = slice(m * 64 + zz * 32, m * 64 + (zz + 1) * 32)
                piece = product[:, zz * HD : (zz + 1) * HD]
                o1[r, at] = piece[0:32]
                sb[r, at] = piece[32:64].astype(BF16)
        send(sb.at[r], rb.at[r], snd.at[16], rb_sem.at[r], partner)

    def finish(r):
        settle(rb.at[r], rb_sem.at[r])
        for half in range(2):
            for b in range(4):
                at = slice((half * 4 + b) * 64, (half * 4 + b + 1) * 64)
                whole = o1[r, at] + rb[r, at].astype(F32)
                if b == 3:
                    t1[r, half] = whole
                else:
                    s1[r, half * 3 + b] = whole.astype(BF16)
                    there = at_x(spots[b][1]) if half else at_y(spots[b][0])
                    send(s1.at[r, half * 3 + b], r1.at[r, half * 3 + b], snd.at[17], r1_sem.at[r], there)

    def reduce_one(r):
        k = r % 4
        settle(r1.at[r], r1_sem.at[r])
        low = iota((16, HD), 1) < 64
        for half in range(2):
            whole = t1[r, half]
            for b in range(3):
                whole = whole + r1[r, half * 3 + b].astype(F32)
            for zz in range(2):
                top, bottom = whole[zz * 32 : zz * 32 + 16], whole[zz * 32 + 16 : zz * 32 + 32]
                fs[r, half, zz, 0] = jnp.where(low, top, pltpu.roll(bottom, 64, 1)).astype(BF16)
                fs[r, half, zz, 1] = jnp.where(low, pltpu.roll(top, 64, 1), bottom).astype(BF16)
            yy, xx = (spots[k][0], x) if half else (y, spots[k][1])
            for zz in range(2):
                owner_z = r // 4 * 4 + half * 2 + zz
                for cc in range(2):

                    def go(zz=zz, cc=cc, owner_z=owner_z):
                        send(
                            fs.at[r, half, zz, cc],
                            fr.at[(c * NZ + z) * 4 + k],
                            snd.at[18],
                            rcv.at[10],
                            (owner_z * NY + yy, xx * NC + cc),
                        )

                    if k == 3:
                        pl.when((owner_z != z) | (cc != c))(go)
                    else:
                        go()

    for r in range(8):
        down(r)
        if r >= 2:
            finish(r - 2)
    for r in range(6, 8):
        finish(r)
    for r in range(4):
        reduce_one(r)
    for r in range(4, 8):
        reduce_one(r)
    fr[(c * NZ + z) * 4 + 3] = fs[z // 4 * 4 + 3, z % 4 // 2, z % 2, c]
    settle(hid.at[0], rcv.at[6])
    settle(fr.at[pl.ds(0, 63)], rcv.at[10])
    for t in range(2):
        added = jnp.sum(fr[t * 32 : (t + 1) * 32].astype(F32), axis=0)
        base = jnp.where(c == 0, hid[t, :, :64], hid[t, :, 64:])
        out[t, 0:16] = (base[0:16] + added[:, :64]).astype(BF16)
        out[t, 16:32] = (base[16:32] + added[:, 64:]).astype(BF16)

    for like, n in (
        (qall.at[pl.ds(0, NS - 1)], 0),
        (ps.at[pl.ds(0, NS - 1)], 1),
        (ss.at[pl.ds(0, NS - 1)], 20),
        (ag.at[pl.ds(0, NS - 1)], 2),
        (hp.at[pl.ds(0, NH - 1)], 3),
        (kv.at[pl.ds(0, 112)], 4),
        (sqz.at[pl.ds(0, NZ - 1)], 5),
        (hid.at[0], 6),
        (ga.at[0, pl.ds(0, 3)], 7),
        (gb.at[0, pl.ds(0, 3)], 8),
        (ga.at[pl.ds(0, 3)], 9),
        (gb.at[pl.ds(0, 3)], 10),
        (ga, 11),
        (gb, 12),
        (sqx.at[pl.ds(0, NX - 1)], 13),
        (sqy.at[pl.ds(0, NY - 1)], 14),
        (sqp.at[0], 15),
        (sb, 16),
        (s1, 17),
        (fr.at[pl.ds(0, 63)], 18),
    ):
        settle(like, snd.at[n])


def shards(
    lengths,
    block_table,
    slot_request,
    kv_pool,
    new_kv,
    queries,
    residual,
    norm_gain,
    w_out,
    w_gate,
    w_up,
    w_down,
):
    vmem = pl.BlockSpec(memory_space=pltpu.VMEM)
    smem = pl.BlockSpec(memory_space=pltpu.SMEM)
    anywhere = pl.BlockSpec(memory_space=pl.ANY)
    scratch = [
        ((NS, 256), jnp.int32),
        ((2, NS, 512), BF16),
        ((1, 512), F32),
        ((TOKENS, 256), BF16),
        ((TOKENS, HD), BF16),
        ((1024, 512), BF16),
        ((104, 16384), BF16),
        ((104, 16384), BF16),
        ((104, 16384), BF16),
        ((NS, ROWS, HD), BF16),
        ((NS * ROWS, HD), BF16),
        ((PAGE, HD), F32),
        ((NS * ROWS, TOKENS), F32),
        ((NS * ROWS, HD), F32),
        ((NS * ROWS, 256), F32),
        ((NS, ROWS, HD), BF16),
        ((NS, ROWS, HD), BF16),
        ((NS, 1, HD), F32),
        ((NS, 1, HD), F32),
        ((NS, ROWS, HD), BF16),
        ((NS * ROWS, HD), F32),
        ((NH, 32, HD), F32),
        ((NH, 32, HD), F32),
        ((2, 32, HD), F32),
        ((NZ, 1, HD), F32),
        ((NX, 1, HD), F32),
        ((NY, 1, HD), F32),
        ((2, 1, HD), F32),
        ((NY, NX, 128, HD), BF16),
        ((NX, NY, 128, HD), BF16),
        ((NY, NX, 128, HD), BF16),
        ((NX, NY, 128, HD), BF16),
        ((8, 512, HD), F32),
        ((8, 512, HD), BF16),
        ((8, 512, HD), BF16),
        ((8, 6, 64, HD), BF16),
        ((8, 6, 64, HD), BF16),
        ((8, 2, 64, HD), F32),
        ((8, 2, 2, 2, 16, HD), BF16),
        ((64, 16, HD), BF16),
    ]
    return pl.pallas_call(
        kernel,
        out_shape=jax.ShapeDtypeStruct((2, NS, 64), BF16),
        in_specs=[smem, smem, vmem, vmem] + [anywhere] * 8,
        out_specs=vmem,
        scratch_shapes=[pltpu.VMEM(shape, kind) for shape, kind in scratch]
        + [
            pltpu.SemaphoreType.DMA(n)
            for n in ((8,), (21,), (14,), (4,), (2, 3), (2, 3), (2, 4, 3), (2, 4, 3), (2, 16), (2, 16), (8,), (8,))
        ],
        compiler_params=pltpu.CompilerParams(
            collective_id=0, has_side_effects=True, vmem_limit_bytes=56 * 1024 * 1024
        ),
    )(
        lengths,
        slot_request,
        new_kv.reshape(3, 256),
        queries.reshape(2, 1024),
        block_table,
        residual,
        norm_gain.reshape(1, 512),
        kv_pool.reshape(TOKENS, 256),
        w_out.reshape(1024, 512),
        w_gate,
        w_up,
        w_down,
    )


def solution(mesh):
    in_specs = (
        P(),
        P(),
        P(),
        P("seq", None, "head", None),
        P(None, "seq", "head", None),
        P(None, "seq", "head", None),
        P(None, None, "seq"),
        P("seq"),
        P("head", None, "seq"),
        P(("seq", "head"), None),
        P(("seq", "head"), None),
        P(("seq", "head"), None),
    )
    out_specs = P(None, None, ("seq", "head"))
    return jax.shard_map(shards, mesh=mesh, in_specs=in_specs, out_specs=out_specs, check_vma=False)
```

```python
import functools
import math

import jax
import jax.numpy as jnp
from jax import lax
from jax.experimental import pallas as pl
from jax.experimental.pallas import tpu as pltpu
from jax.sharding import PartitionSpec as P

EPSILON = 1e-05
NZ, NY, NX, NC = 8, 4, 4, 2
NS, NH = NZ * NY, NX * NC
HD = 128
PAGE = 64
ROWS = 16
TOKENS = 4096
CHUNK = 512
APART = (0, 1, 2, 3, 7, 6, 5, 4)
LAG = 12
BATCH, LAST_BATCH = 12, 8
FAR = 131072.0
F32, BF16 = jnp.float32, jnp.bfloat16
NT = (((1,), (1,)), ((), ()))
EXP_SCALE = math.log2(math.e) / math.sqrt(HD)


RING = (1, 3, 2)
NEAR = sorted(
    ((dz, dy) for dz in range(NZ) for dy in range(NY)),
    key=lambda d: min(d[0], NZ - d[0]) + min(d[1], NY - d[1]),
)
SEEN = [NEAR.index(((NZ - dz) % NZ, (NY - dy) % NY)) for dz, dy in NEAR]
AROUND = NEAR[:0:-1]
HALF = NS // 2


def iota(shape, dim):
    return lax.broadcasted_iota(jnp.int32, shape, dim)


def kernel(
    lengths_hbm, slot_hbm, new_hbm, queries_hbm, table_hbm, residual_hbm, gain_hbm, kv_hbm, wo_hbm, wg_hbm, wu_hbm, wd_hbm,
    out,
    lengths, slot_request, new_kv, queries, table, residual, gain, kv, bias, wo, wg, wu, wd,
    qall, hot, codes, scores, peak, acc,
    ps, pr, ss, sr, ag, af, hp, hr, hid,
    sqz, sqx, sqy, sqp, ga, gb, pa, pb,
    o1, sb, rb, s1, r1, t1, fs, fr,
    load_sem, snd, rcv, z_sem, a2, b2, a3, b3, pa_sem, pb_sem, rb_sem, r1_sem,
):
    s = lax.axis_index("seq")
    h = lax.axis_index("head")
    z, y = s // NY, s % NY
    x, c = h // NC, h % NC
    partner = (s, x * NC + 1 - c)

    def shard(dz, dy):
        return ((z + dz) % NZ) * NY + (y + dy) % NY

    def at_y(other):
        return (z * NY + other, h)

    def at_x(other):
        return (s, other * NC + c)

    def send(src, dst, send_sem, recv_sem, device):
        pltpu.make_async_remote_copy(
            src_ref=src,
            dst_ref=dst,
            send_sem=send_sem,
            recv_sem=recv_sem,
            device_id=device,
            device_id_type=pl.DeviceIdType.MESH,
        ).start()

    def settle(like, sem):
        pltpu.make_async_copy(like, like, sem).wait()

    barrier = pltpu.get_barrier_semaphore()

    def greet(device):
        pl.semaphore_signal(barrier, inc=1, device_id=device, device_id_type=pl.DeviceIdType.MESH)

    for dz, dy in AROUND:
        greet((shard(dz, dy), h))

    @pl.loop(1, NH)
    def _(d):
        greet((s, (h + d) % NH))

    @pl.loop(1, NZ)
    def _(d):
        greet((((z + d) % NZ) * NY + y, x * NC + 1 - c))

    loads = [
        pltpu.make_async_copy(src, dst, load_sem.at[n])
        for n, (src, dst) in enumerate(
            (
                (kv_hbm, kv),
                (wo_hbm, wo),
                (wg_hbm, wg),
                (wu_hbm, wu),
                (wd_hbm, wd),
                (table_hbm, table),
                (residual_hbm, residual),
                (gain_hbm, gain),
                (lengths_hbm, lengths),
                (slot_hbm, slot_request),
                (new_hbm, new_kv),
                (queries_hbm, queries),
            )
        )
    ]
    for n in (11, 8, 9, 5, 0, 10, 1, 6, 7, 2, 3, 4):
        loads[n].start()

    loads[11].wait()
    wide = queries[...].astype(F32)
    own_query = jnp.concatenate(
        [wide[t : t + 1, g * HD : (g + 1) * HD] for t in range(2) for g in range(8)], axis=0
    )
    qall[0] = own_query.astype(BF16)

    pl.semaphore_wait(barrier, (NS - 1) + (NH - 1) + (NZ - 1))

    for n in range(1, NS):
        m = SEEN[n]
        send(qall.at[0], qall.at[m], snd.at[0], rcv.at[0 if m < HALF else 14], (shard(*NEAR[n]), h))

    for n in (8, 9, 5):
        loads[n].wait()
    row = iota((NS, HD), 0)
    length = jnp.zeros((NS, HD), jnp.int32)
    slot = jnp.zeros((NS, HD), jnp.int32)
    for r in range(NS):
        length = jnp.where(row == r, lengths[r], length)
        slot = jnp.where(row == slot_request[shard(*NEAR[r])], r, slot)
    halves = []
    for half in range(2):
        page = iota((NS, HD), 1) + half * HD
        filled = jnp.clip(length - page * PAGE, 0, PAGE)
        local = jnp.where(filled > 0, table[:, half * HD : (half + 1) * HD] - s * PAGE, -1)
        halves.append((local, (slot * HD + filled).astype(F32)))

    def find(p, carry):
        hits = [jnp.where(local == p, code, 0.0) for local, code in halves]
        codes[pl.ds(p, 1), :] = jnp.sum(hits[0] + hits[1], axis=0, keepdims=True)
        return carry

    lax.fori_loop(0, PAGE, find, 0, unroll=4)
    code = jnp.sum(codes[...], axis=1, keepdims=True)
    codes[...] = jnp.broadcast_to(code, (PAGE, HD))

    def cover(p, carry):
        both = codes[pl.ds(p, 1), :].astype(jnp.int32)
        mine = (iota((PAGE, HD), 1) == both // HD) & (iota((PAGE, HD), 0) < both % HD)
        bias[pl.ds(pl.multiple_of(p * PAGE, PAGE), PAGE), :] = jnp.where(mine, 0.0, -FAR).astype(BF16)
        return carry

    lax.fori_loop(0, PAGE, cover, 0, unroll=4)
    hot[...] = jnp.where(iota((NS * ROWS, HD), 0) // ROWS == iota((NS * ROWS, HD), 1), 1.0, 0.0).astype(BF16)

    def attend(half):
        slots = slice(half * HALF, (half + 1) * HALF)
        rows = slice(half * HALF * ROWS, (half + 1) * HALF * ROWS)
        count = HALF * ROWS
        aug_query = jnp.concatenate([qall[slots].reshape(count, HD), hot[rows]], axis=1)
        peak[rows] = jnp.full((count, HD), -4.0 * FAR, F32)
        for k in range(TOKENS // CHUNK):
            tokens = slice(k * CHUNK, (k + 1) * CHUNK)
            aug_key = jnp.concatenate([kv[tokens, :HD], bias[tokens]], axis=1)
            raw = lax.dot_general(aug_query, aug_key, NT, preferred_element_type=F32)
            scores[rows, tokens] = raw
            best = functools.reduce(jnp.maximum, [raw[:, n : n + HD] for n in range(0, CHUNK, HD)])
            peak[rows] = jnp.maximum(peak[rows], best)
        top = jnp.max(peak[rows], axis=1, keepdims=True)
        peak[rows] = jnp.broadcast_to(top, (count, HD))
        acc[rows] = jnp.zeros((count, 2 * HD), F32)
        for k in range(TOKENS // CHUNK):
            tokens = slice(k * CHUNK, (k + 1) * CHUNK)
            aug_value = jnp.concatenate([kv[tokens, HD:], jnp.ones((CHUNK, HD), BF16)], axis=1)
            base = jnp.concatenate([peak[rows]] * (CHUNK // HD), axis=1)
            weights = jnp.exp2((scores[rows, tokens] - base) * EXP_SCALE).astype(BF16)
            acc[rows] += jnp.dot(weights, aug_value, preferred_element_type=F32)
        cube = (HALF, ROWS, HD)
        ps[slots] = acc[rows, :HD].astype(BF16).reshape(cube)
        lane, line = iota(cube, 2), iota(cube, 1)
        stats = jnp.where(lane == line, peak[rows].reshape(cube), 0.0)
        stats = jnp.where(lane == line + ROWS, acc[rows, HD:].reshape(cube), stats)
        ss[slots] = jnp.sum(stats, axis=1, keepdims=True)
        if half == 0:
            pr[0] = ps[0]
            sr[0] = ss[0]
        for n in range((half + 1) * HALF - 1, max(half * HALF, 1) - 1, -1):
            there = (shard(*NEAR[n]), h)
            send(ps.at[n], pr.at[SEEN[n]], snd.at[1], rcv.at[1], there)
            send(ss.at[n], sr.at[SEEN[n]], snd.at[20], rcv.at[13], there)

    loads[0].wait()
    settle(qall.at[pl.ds(1, HALF - 1)], rcv.at[0])
    attend(0)
    settle(qall.at[pl.ds(HALF, HALF)], rcv.at[14])
    attend(1)
    cube = (NS, ROWS, HD)
    lane, line = iota(cube, 2), iota(cube, 1)

    loads[10].wait()
    fresh = new_kv[...].astype(F32)
    late = iota((ROWS, 1), 0) >= ROWS // 2
    rounded_query = own_query.astype(BF16).astype(F32)
    fresh_scores = []
    for e in range(3):
        raw = jnp.sum(rounded_query * fresh[e : e + 1, :HD], axis=1, keepdims=True)
        fresh_scores.append(jnp.where(late, raw, -FAR) if e == 2 else raw)
    settle(pr.at[pl.ds(0, NS - 1)], rcv.at[1])
    settle(sr.at[pl.ds(0, NS - 1)], rcv.at[13])
    stats = jnp.broadcast_to(sr[...], cube)
    tops = jnp.sum(jnp.where(lane == line, stats, 0.0), axis=2, keepdims=True)
    sums = jnp.sum(jnp.where(lane == line + ROWS, stats, 0.0), axis=2, keepdims=True)
    top = jnp.max(tops, axis=0)
    for raw in fresh_scores:
        top = jnp.maximum(top, raw)
    factor = jnp.exp2((tops - top[None]) * EXP_SCALE)
    total = jnp.sum(factor * sums, axis=0)
    mixed = jnp.sum(factor * pr[...].astype(F32), axis=0)
    for e, raw in enumerate(fresh_scores):
        weight = jnp.exp2((raw - top) * EXP_SCALE).astype(BF16).astype(F32)
        total = total + weight
        mixed = mixed + weight * fresh[e : e + 1, HD:]
    ag[s] = (mixed / total).astype(BF16)

    for dz, dy in AROUND:
        send(ag.at[s], ag.at[s], snd.at[2], rcv.at[2], (shard(dz, dy), h))

    loads[1].wait()
    loads[6].wait()
    loads[7].wait()
    settle(ag.at[pl.ds(0, NS - 1)], rcv.at[2])

    af[...] = ag[...].reshape(NS * ROWS, HD).astype(F32)
    attended = jnp.concatenate(
        [
            jnp.concatenate([af[pl.ds(t * 8 + g, NS, stride=ROWS), :] for g in range(8)], axis=1)
            for t in range(2)
        ],
        axis=0,
    ).astype(BF16)
    part = jnp.dot(attended, wo[...], preferred_element_type=F32)
    for xx in range(NX):
        for cc in range(NC):
            piece = part[cc * NS : (cc + 1) * NS, xx * HD : (xx + 1) * HD]
            hp[xx * NC + cc] = piece.astype(BF16)
    hr[h] = hp[h]

    @pl.loop(1, NH)
    def _(d):
        other = (h + d) % NH
        send(hp.at[other], hr.at[h], snd.at[3], rcv.at[3], (s, other))

    columns = pl.ds(pl.multiple_of(x * HD, HD), HD)
    settle(hr.at[pl.ds(0, NH - 1)], rcv.at[3])
    hidden = residual[c, :, columns].astype(F32) + jnp.sum(hr[...].astype(F32), axis=0)
    hid[c] = hidden
    square = jnp.sum(hidden * hidden, axis=1, keepdims=True)
    halves = ((ga, pa, a2, a3, pa_sem, x, y, at_x, at_y), (gb, pb, b2, b3, pb_sem, y, x, at_y, at_x))
    ga[y, x, 0:32] = (hidden * gain[:, columns]).astype(BF16)
    spread = jnp.where(iota((NS, HD), 0) == iota((NS, HD), 1), square, 0.0)
    sqz[z] = jnp.sum(spread, axis=0, keepdims=True)
    own = ga.at[y, x, pl.ds(0, 32)]
    for p in range(1, NZ):
        there = (((z + NZ - APART[p]) % NZ) * NY + y, h)
        place = ga.at[y, x, pl.ds(p * 32, 32)] if p < 4 else gb.at[x, y, pl.ds((p - 4) * 32, 32)]
        send(own, place, snd.at[4], z_sem.at[p // 2], there)
    for d in (4, 3, 5, 2, 6, 1, 7):
        there = (((z + d) % NZ) * NY + y, h)
        send(sqz.at[z], sqz.at[z], snd.at[5], rcv.at[5], there)
    send(hid.at[c], hid.at[c], snd.at[6], rcv.at[6], partner)
    done = []

    def block(ref, outer, inner, w):
        return ref.at[outer, inner, pl.ds(w * 64, 64)]

    def pass_on(half, w, inner, n):
        full, _, _, last, _, _, outer, _, at_last = halves[half]
        here = block(full, outer, inner, w)
        for d in RING:
            send(here, here, snd.at[9 + half], last.at[w, n, d - 1], at_last((outer + d) % 4))
        cross(half, w, outer, inner, n)

    def cross(half, w, outer, inner, n):
        full, other, _, _, sem, _, _, _, _ = halves[half]
        send(block(full, outer, inner, w), block(other, outer, inner, w), snd.at[11 + half], sem.at[w, n], partner)
        done.append((half, w, outer, inner, n))

    for w in range(2):
        for half in range(2):
            full, _, first, _, _, inner, outer, at_first, _ = halves[half]
            here = block(full, outer, inner, w)
            if half == 0 and w == 0:
                settle(own, z_sem.at[0])
            else:
                settle(here, z_sem.at[half * 2 + w])
            for d in RING:
                send(here, here, snd.at[7 + half], first.at[w, d - 1], at_first((inner + d) % 4))
            pass_on(half, w, inner, 0)
    settle(sqz.at[pl.ds(0, NZ - 1)], rcv.at[5])
    sqx[x] = jnp.sum(sqz[...], axis=0)
    for d in RING:
        send(sqx.at[x], sqx.at[x], snd.at[13], rcv.at[7], at_x((x + d) % NX))

    loads[2].wait()
    loads[3].wait()

    def multiply(items, sums):
        for half, w, outer, inner, n in items:
            full, other, _, _, sem, _, _, _, _ = halves[half]
            settle(block(other, outer, inner, w), sem.at[w, n])
        gate, up = sums
        for half, w, outer, inner, n in items:
            full, other, _, _, _, _, _, _, _ = halves[half]
            yy, xx = (inner, outer) if half else (outer, inner)
            both = (2 * w, 2 * w + 1)
            stream = jnp.concatenate(
                [
                    jnp.concatenate([ref[outer, inner, p * 32 : (p + 1) * 32] for p in both], axis=1)
                    for ref in (full, other)
                ],
                axis=0,
            )
            zs = [(z + APART[half * 4 + p]) % NZ for p in both]
            where = [pl.ds(pl.multiple_of(zz * 2048 + yy * 512 + xx * HD, HD), HD) for zz in zs]
            left = [jnp.concatenate([ref[:, at] for at in where], axis=1) for ref in (wg, wu)]
            gate = gate + lax.dot_general(left[0], stream, NT, preferred_element_type=F32)
            up = up + lax.dot_general(left[1], stream, NT, preferred_element_type=F32)
        return gate, up

    def catch_up(lag, batch, sums):
        while len(done) >= lag + batch:
            sums = multiply([done.pop(0) for _ in range(batch)], sums)
        return sums

    sums = (jnp.zeros((104, 64), F32), jnp.zeros((104, 64), F32))

    def last_arrivals(w, half, n, k):
        full, _, _, last, _, inner, outer, _, _ = halves[half]
        for d in RING:
            there, beside = (outer + 4 - d) % 4, (inner + 4 - k) % 4
            settle(block(full, there, beside, w), last.at[w, n, d - 1])
            cross(half, w, there, beside, 3 * n + 3 + d)

    for w in range(2):
        for half in range(2):
            full, _, first, _, _, inner, outer, _, _ = halves[half]
            for n, d in enumerate(RING):
                beside = (inner + 4 - d) % 4
                settle(block(full, outer, beside, w), first.at[w, d - 1])
                pass_on(half, w, beside, n + 1)
        for half in range(2):
            last_arrivals(w, half, 0, 0)
    settle(sqx.at[pl.ds(0, NX - 1)], rcv.at[7])
    sqy[y] = jnp.sum(sqx[...], axis=0)
    for d in RING:
        send(sqy.at[y], sqy.at[y], snd.at[14], rcv.at[8], at_y((y + d) % NY))
    sums = catch_up(LAG, BATCH, sums)
    for w in range(2):
        for n, k in enumerate(RING):
            for half in range(2):
                last_arrivals(w, half, n + 1, k)
                sums = catch_up(LAG, BATCH, sums)
        if w == 0:
            settle(sqy.at[pl.ds(0, NY - 1)], rcv.at[8])
            sqp[0] = jnp.sum(sqy[...], axis=0)
            send(sqp.at[0], sqp.at[1], snd.at[15], rcv.at[9], partner)
    sums = catch_up(LAST_BATCH, BATCH, sums)
    while done:
        sums = catch_up(0, min(LAST_BATCH, len(done)), sums)
    settle(sqp.at[0], rcv.at[9])
    square = jnp.broadcast_to(sqp[0], (8, HD)) + pltpu.roll(jnp.broadcast_to(sqp[1], (8, HD)), 32, 1)
    scale = lax.rsqrt(square[0:1, 0:64] * (1.0 / 16384.0) + EPSILON)
    gate = sums[0] * scale
    up = sums[1] * scale
    activation = (gate / (1.0 + jnp.exp(-gate)) * up).T.astype(BF16)

    loads[4].wait()
    turn = (2, 1, 3, 0)
    spots = [[(y + b) % NY, (x + b) % NX] for b in turn]

    def groups(r):
        k, first = r % 4, r // 4 * 4
        return [(spots[b][0], spots[k][1], first) for b in range(4)] + [
            (spots[k][0], spots[b][1], first + 2) for b in range(4)
        ]

    def down(r):
        for m, (yy, xx, first) in enumerate(groups(r)):
            weight = jnp.concatenate(
                [
                    wd[:, pl.ds(pl.multiple_of((first + zz) * 2048 + yy * 512 + xx * HD, HD), HD)]
                    for zz in range(2)
                ],
                axis=1,
            )
            product = jnp.dot(activation, weight, preferred_element_type=F32)
            for zz in range(2):
                at = slice(m * 64 + zz * 32, m * 64 + (zz + 1) * 32)
                piece = product[:, zz * HD : (zz + 1) * HD]
                o1[r, at] = piece[0:32]
                sb[r, at] = piece[32:64].astype(BF16)
        send(sb.at[r], rb.at[r], snd.at[16], rb_sem.at[r], partner)

    def finish(r):
        settle(rb.at[r], rb_sem.at[r])
        for half in range(2):
            for b in range(4):
                at = slice((half * 4 + b) * 64, (half * 4 + b + 1) * 64)
                whole = o1[r, at] + rb[r, at].astype(F32)
                if b == 3:
                    t1[r, half] = whole
                else:
                    s1[r, half * 3 + b] = whole.astype(BF16)
                    there = at_x(spots[b][1]) if half else at_y(spots[b][0])
                    send(s1.at[r, half * 3 + b], r1.at[r, half * 3 + b], snd.at[17], r1_sem.at[r], there)

    def reduce_one(r):
        k = r % 4
        settle(r1.at[r], r1_sem.at[r])
        low = iota((16, HD), 1) < 64
        for half in range(2):
            whole = t1[r, half]
            for b in range(3):
                whole = whole + r1[r, half * 3 + b].astype(F32)
            for zz in range(2):
                top, bottom = whole[zz * 32 : zz * 32 + 16], whole[zz * 32 + 16 : zz * 32 + 32]
                fs[r, half, zz, 0] = jnp.where(low, top, pltpu.roll(bottom, 64, 1)).astype(BF16)
                fs[r, half, zz, 1] = jnp.where(low, pltpu.roll(top, 64, 1), bottom).astype(BF16)
            yy, xx = (spots[k][0], x) if half else (y, spots[k][1])
            for zz in range(2):
                owner_z = r // 4 * 4 + half * 2 + zz
                for cc in range(2):

                    def go(zz=zz, cc=cc, owner_z=owner_z):
                        send(
                            fs.at[r, half, zz, cc],
                            fr.at[(c * NZ + z) * 4 + k],
                            snd.at[18],
                            rcv.at[10],
                            (owner_z * NY + yy, xx * NC + cc),
                        )

                    if k == 3:
                        pl.when((owner_z != z) | (cc != c))(go)
                    else:
                        go()

    for r in range(8):
        down(r)
        if r >= 2:
            finish(r - 2)
    for r in range(6, 8):
        finish(r)
    for r in range(4):
        reduce_one(r)
    for r in range(4, 8):
        reduce_one(r)
    fr[(c * NZ + z) * 4 + 3] = fs[z // 4 * 4 + 3, z % 4 // 2, z % 2, c]
    settle(hid.at[0], rcv.at[6])
    settle(fr.at[pl.ds(0, 63)], rcv.at[10])
    for t in range(2):
        added = jnp.sum(fr[t * 32 : (t + 1) * 32].astype(F32), axis=0)
        base = jnp.where(c == 0, hid[t, :, :64], hid[t, :, 64:])
        out[t, 0:16] = base[0:16] + added[:, :64]
        out[t, 16:32] = base[16:32] + added[:, 64:]

    for like, n in (
        (qall.at[pl.ds(0, NS - 1)], 0),
        (ps.at[pl.ds(0, NS - 1)], 1),
        (ss.at[pl.ds(0, NS - 1)], 20),
        (ag.at[pl.ds(0, NS - 1)], 2),
        (hp.at[pl.ds(0, NH - 1)], 3),
        (kv.at[pl.ds(0, 112)], 4),
        (sqz.at[pl.ds(0, NZ - 1)], 5),
        (hid.at[0], 6),
        (ga.at[0, pl.ds(0, 3)], 7),
        (gb.at[0, pl.ds(0, 3)], 8),
        (ga.at[pl.ds(0, 3)], 9),
        (gb.at[pl.ds(0, 3)], 10),
        (ga, 11),
        (gb, 12),
        (sqx.at[pl.ds(0, NX - 1)], 13),
        (sqy.at[pl.ds(0, NY - 1)], 14),
        (sqp.at[0], 15),
        (sb, 16),
        (s1, 17),
        (fr.at[pl.ds(0, 63)], 18),
    ):
        settle(like, snd.at[n])


def shards(
    lengths,
    block_table,
    slot_request,
    kv_pool,
    new_kv,
    queries,
    residual,
    norm_gain,
    w_out,
    w_gate,
    w_up,
    w_down,
):
    vmem = pl.BlockSpec(memory_space=pltpu.VMEM)
    anywhere = pl.BlockSpec(memory_space=pl.ANY)
    scratch = [
        ((3, 256), BF16),
        ((2, 1024), BF16),
        ((NS, 256), jnp.int32),
        ((2, NS, 512), BF16),
        ((1, 512), F32),
        ((TOKENS, 256), BF16),
        ((TOKENS, HD), BF16),
        ((1024, 512), BF16),
        ((104, 16384), BF16),
        ((104, 16384), BF16),
        ((104, 16384), BF16),
        ((NS, ROWS, HD), BF16),
        ((NS * ROWS, HD), BF16),
        ((PAGE, HD), F32),
        ((NS * ROWS, TOKENS), F32),
        ((NS * ROWS, HD), F32),
        ((NS * ROWS, 256), F32),
        ((NS, ROWS, HD), BF16),
        ((NS, ROWS, HD), BF16),
        ((NS, 1, HD), F32),
        ((NS, 1, HD), F32),
        ((NS, ROWS, HD), BF16),
        ((NS * ROWS, HD), F32),
        ((NH, 32, HD), BF16),
        ((NH, 32, HD), BF16),
        ((2, 32, HD), F32),
        ((NZ, 1, HD), F32),
        ((NX, 1, HD), F32),
        ((NY, 1, HD), F32),
        ((2, 1, HD), F32),
        ((NY, NX, 128, HD), BF16),
        ((NX, NY, 128, HD), BF16),
        ((NY, NX, 128, HD), BF16),
        ((NX, NY, 128, HD), BF16),
        ((8, 512, HD), F32),
        ((8, 512, HD), BF16),
        ((8, 512, HD), BF16),
        ((8, 6, 64, HD), BF16),
        ((8, 6, 64, HD), BF16),
        ((8, 2, 64, HD), F32),
        ((8, 2, 2, 2, 16, HD), BF16),
        ((64, 16, HD), BF16),
    ]
    return pl.pallas_call(
        kernel,
        out_shape=jax.ShapeDtypeStruct((2, NS, 64), F32),
        in_specs=[anywhere] * 12,
        out_specs=vmem,
        scratch_shapes=[pltpu.SMEM((NS,), jnp.int32)] * 2
        + [pltpu.VMEM(shape, kind) for shape, kind in scratch]
        + [
            pltpu.SemaphoreType.DMA(n)
            for n in ((12,), (21,), (15,), (4,), (2, 3), (2, 3), (2, 4, 3), (2, 4, 3), (2, 16), (2, 16), (8,), (8,))
        ],
        compiler_params=pltpu.CompilerParams(
            collective_id=0, has_side_effects=True, vmem_limit_bytes=56 * 1024 * 1024
        ),
    )(
        lengths,
        slot_request,
        new_kv.reshape(3, 256),
        queries.reshape(2, 1024),
        block_table,
        residual,
        norm_gain.reshape(1, 512),
        kv_pool.reshape(TOKENS, 256),
        w_out.reshape(1024, 512),
        w_gate,
        w_up,
        w_down,
    ).astype(BF16)


def solution(mesh):
    in_specs = (
        P(),
        P(),
        P(),
        P("seq", None, "head", None),
        P(None, "seq", "head", None),
        P(None, "seq", "head", None),
        P(None, None, "seq"),
        P("seq"),
        P("head", None, "seq"),
        P(("seq", "head"), None),
        P(("seq", "head"), None),
        P(("seq", "head"), None),
    )
    out_specs = P(None, None, ("seq", "head"))
    return jax.shard_map(shards, mesh=mesh, in_specs=in_specs, out_specs=out_specs, check_vma=False)
```

```python
import functools
import math

import jax
import jax.numpy as jnp
from jax import lax
from jax.experimental import pallas as pl
from jax.experimental.pallas import tpu as pltpu
from jax.sharding import PartitionSpec as P

EPSILON = 1e-05
NZ, NY, NX, NC = 8, 4, 4, 2
NS, NH = NZ * NY, NX * NC
HD = 128
PAGE = 64
ROWS = 16
TOKENS = 4096
CHUNK = 512
WIDE = 2048
APART = (0, 1, 2, 3, 7, 6, 5, 4)
LAG = 16
BATCH, LAST_BATCH = 4, 4
FAR = 131072.0
F32, BF16 = jnp.float32, jnp.bfloat16
NT = (((1,), (1,)), ((), ()))
EXP_SCALE = math.log2(math.e) / math.sqrt(HD)


OUT = (2, 1, 3)
RING = (1, 3, 2)
NEAR = sorted(
    ((dz, dy) for dz in range(NZ) for dy in range(NY)),
    key=lambda d: min(d[0], NZ - d[0]) + min(d[1], NY - d[1]),
)
SEEN = [NEAR.index(((NZ - dz) % NZ, (NY - dy) % NY)) for dz, dy in NEAR]
AROUND = NEAR[:0:-1]
HALF = NS // 2


def iota(shape, dim):
    return lax.broadcasted_iota(jnp.int32, shape, dim)


def kernel(
    lengths_hbm, slot_hbm, new_hbm, queries_hbm, table_hbm, residual_hbm, gain_hbm, kv_hbm, wo_hbm, wg_hbm, wu_hbm, wd_hbm,
    out,
    lengths, slot_request, new_kv, queries, table, residual, gain, kv, bias, wo, wg, wu, wd,
    qall, hot, codes, scores, peak, acc,
    ps, pr, ss, sr, ag, af, hp, hr, hid,
    sqz, sqx, sqy, sqp, ga, gb, pa, pb,
    o1, sb, rb, s1, r1, t1, fs, fr,
    load_sem, snd, rcv, z_sem, a2, b2, a3, b3, pa_sem, pb_sem, rb_sem, r1_sem,
):
    s = lax.axis_index("seq")
    h = lax.axis_index("head")
    z, y = s // NY, s % NY
    x, c = h // NC, h % NC
    partner = (s, x * NC + 1 - c)

    def shard(dz, dy):
        return ((z + dz) % NZ) * NY + (y + dy) % NY

    def at_y(other):
        return (z * NY + other, h)

    def at_x(other):
        return (s, other * NC + c)

    def send(src, dst, send_sem, recv_sem, device):
        pltpu.make_async_remote_copy(
            src_ref=src,
            dst_ref=dst,
            send_sem=send_sem,
            recv_sem=recv_sem,
            device_id=device,
            device_id_type=pl.DeviceIdType.MESH,
        ).start()

    def settle(like, sem):
        pltpu.make_async_copy(like, like, sem).wait()

    barrier = pltpu.get_barrier_semaphore()

    def greet(device):
        pl.semaphore_signal(barrier, inc=1, device_id=device, device_id_type=pl.DeviceIdType.MESH)

    for dz, dy in AROUND:
        greet((shard(dz, dy), h))

    @pl.loop(1, NH)
    def _(d):
        greet((s, (h + d) % NH))

    @pl.loop(1, NZ)
    def _(d):
        greet((((z + d) % NZ) * NY + y, x * NC + 1 - c))

    loads = [
        pltpu.make_async_copy(src, dst, load_sem.at[n])
        for n, (src, dst) in enumerate(
            (
                (kv_hbm, kv),
                (wo_hbm, wo),
                (wg_hbm, wg),
                (wu_hbm, wu),
                (wd_hbm, wd),
                (table_hbm, table),
                (residual_hbm, residual),
                (gain_hbm, gain),
                (lengths_hbm, lengths),
                (slot_hbm, slot_request),
                (new_hbm, new_kv),
                (queries_hbm, queries),
            )
        )
    ]
    for n in (11, 8, 9, 5, 0, 10, 1, 6, 7, 2, 3, 4):
        loads[n].start()

    loads[11].wait()
    wide = queries[...].astype(F32)
    own_query = jnp.concatenate(
        [wide[t : t + 1, g * HD : (g + 1) * HD] for t in range(2) for g in range(8)], axis=0
    )
    qall[0] = own_query.astype(BF16)

    pl.semaphore_wait(barrier, (NS - 1) + (NH - 1) + (NZ - 1))

    for n in range(1, NS):
        m = SEEN[n]
        send(qall.at[0], qall.at[m], snd.at[0], rcv.at[0 if m < HALF else 14], (shard(*NEAR[n]), h))

    for n in (8, 9, 5):
        loads[n].wait()
    row = iota((NS, HD), 0)
    length = jnp.zeros((NS, HD), jnp.int32)
    slot = jnp.zeros((NS, HD), jnp.int32)
    for r in range(NS):
        length = jnp.where(row == r, lengths[r], length)
        slot = jnp.where(row == slot_request[shard(*NEAR[r])], r, slot)
    halves = []
    for half in range(2):
        page = iota((NS, HD), 1) + half * HD
        filled = jnp.clip(length - page * PAGE, 0, PAGE)
        local = jnp.where(filled > 0, table[:, half * HD : (half + 1) * HD] - s * PAGE, -1)
        halves.append((local, (slot * HD + filled).astype(F32)))

    def find(p, carry):
        hits = [jnp.where(local == p, code, 0.0) for local, code in halves]
        codes[pl.ds(p, 1), :] = jnp.sum(hits[0] + hits[1], axis=0, keepdims=True)
        return carry

    lax.fori_loop(0, PAGE, find, 0, unroll=4)
    code = jnp.sum(codes[...], axis=1, keepdims=True)
    codes[...] = jnp.broadcast_to(code, (PAGE, HD))

    def cover(p, carry):
        both = codes[pl.ds(p, 1), :].astype(jnp.int32)
        mine = (iota((PAGE, HD), 1) == both // HD) & (iota((PAGE, HD), 0) < both % HD)
        bias[pl.ds(pl.multiple_of(p * PAGE, PAGE), PAGE), :] = jnp.where(mine, 0.0, -FAR).astype(BF16)
        return carry

    lax.fori_loop(0, PAGE, cover, 0, unroll=4)
    hot[...] = jnp.where(iota((NS * ROWS, HD), 0) // ROWS == iota((NS * ROWS, HD), 1), 1.0, 0.0).astype(BF16)

    def attend(half):
        slots = slice(half * HALF, (half + 1) * HALF)
        rows = slice(half * HALF * ROWS, (half + 1) * HALF * ROWS)
        count = HALF * ROWS
        aug_query = jnp.concatenate([qall[slots].reshape(count, HD), hot[rows]], axis=1)
        peak[rows] = jnp.full((count, HD), -4.0 * FAR, F32)
        for k in range(TOKENS // CHUNK):
            tokens = slice(k * CHUNK, (k + 1) * CHUNK)
            aug_key = jnp.concatenate([kv[tokens, :HD], bias[tokens]], axis=1)
            raw = lax.dot_general(aug_query, aug_key, NT, preferred_element_type=F32)
            scores[rows, tokens] = raw
            best = functools.reduce(jnp.maximum, [raw[:, n : n + HD] for n in range(0, CHUNK, HD)])
            peak[rows] = jnp.maximum(peak[rows], best)
        top = jnp.max(peak[rows], axis=1, keepdims=True)
        peak[rows] = jnp.broadcast_to(top, (count, HD))
        total = jnp.zeros((count, 2 * HD), F32)
        for k in range(TOKENS // WIDE):
            tokens = slice(k * WIDE, (k + 1) * WIDE)
            aug_value = jnp.concatenate([kv[tokens, HD:], jnp.ones((WIDE, HD), BF16)], axis=1)
            base = jnp.concatenate([peak[rows]] * (WIDE // HD), axis=1)
            weights = jnp.exp2((scores[rows, tokens] - base) * EXP_SCALE).astype(BF16)
            total = total + jnp.dot(weights, aug_value, preferred_element_type=F32)
        acc[rows] = total
        cube = (HALF, ROWS, HD)
        ps[slots] = acc[rows, :HD].astype(BF16).reshape(cube)
        lane, line = iota(cube, 2), iota(cube, 1)
        stats = jnp.where(lane == line, peak[rows].reshape(cube), 0.0)
        stats = jnp.where(lane == line + ROWS, acc[rows, HD:].reshape(cube), stats)
        ss[slots] = jnp.sum(stats, axis=1, keepdims=True)
        if half == 0:
            pr[0] = ps[0]
            sr[0] = ss[0]
        for n in range((half + 1) * HALF - 1, max(half * HALF, 1) - 1, -1):
            there = (shard(*NEAR[n]), h)
            send(ps.at[n], pr.at[SEEN[n]], snd.at[1], rcv.at[1], there)
            send(ss.at[n], sr.at[SEEN[n]], snd.at[20], rcv.at[13], there)

    loads[0].wait()
    settle(qall.at[pl.ds(1, HALF - 1)], rcv.at[0])
    attend(0)
    settle(qall.at[pl.ds(HALF, HALF)], rcv.at[14])
    attend(1)
    cube = (NS, ROWS, HD)
    lane, line = iota(cube, 2), iota(cube, 1)

    loads[10].wait()
    fresh = new_kv[...].astype(F32)
    late = iota((ROWS, 1), 0) >= ROWS // 2
    rounded_query = own_query.astype(BF16).astype(F32)
    fresh_scores = []
    for e in range(3):
        raw = jnp.sum(rounded_query * fresh[e : e + 1, :HD], axis=1, keepdims=True)
        fresh_scores.append(jnp.where(late, raw, -FAR) if e == 2 else raw)
    settle(pr.at[pl.ds(0, NS - 1)], rcv.at[1])
    settle(sr.at[pl.ds(0, NS - 1)], rcv.at[13])
    stats = jnp.broadcast_to(sr[...], cube)
    tops = jnp.sum(jnp.where(lane == line, stats, 0.0), axis=2, keepdims=True)
    sums = jnp.sum(jnp.where(lane == line + ROWS, stats, 0.0), axis=2, keepdims=True)
    top = jnp.max(tops, axis=0)
    for raw in fresh_scores:
        top = jnp.maximum(top, raw)
    factor = jnp.exp2((tops - top[None]) * EXP_SCALE)
    total = jnp.sum(factor * sums, axis=0)
    mixed = jnp.sum(factor * pr[...].astype(F32), axis=0)
    for e, raw in enumerate(fresh_scores):
        weight = jnp.exp2((raw - top) * EXP_SCALE).astype(BF16).astype(F32)
        total = total + weight
        mixed = mixed + weight * fresh[e : e + 1, HD:]
    ag[s] = (mixed / total).astype(BF16)

    for dz, dy in AROUND:
        send(ag.at[s], ag.at[s], snd.at[2], rcv.at[2], (shard(dz, dy), h))

    loads[1].wait()
    loads[6].wait()
    loads[7].wait()
    settle(ag.at[pl.ds(0, NS - 1)], rcv.at[2])

    af[...] = ag[...].reshape(NS * ROWS, HD).astype(F32)
    attended = jnp.concatenate(
        [
            jnp.concatenate([af[pl.ds(t * 8 + g, NS, stride=ROWS), :] for g in range(8)], axis=1)
            for t in range(2)
        ],
        axis=0,
    ).astype(BF16)
    part = jnp.dot(attended, wo[...], preferred_element_type=F32)
    for xx in range(NX):
        for cc in range(NC):
            piece = part[cc * NS : (cc + 1) * NS, xx * HD : (xx + 1) * HD]
            hp[xx * NC + cc] = piece.astype(BF16)
    hr[h] = hp[h]

    @pl.loop(1, NH)
    def _(d):
        other = (h + d) % NH
        send(hp.at[other], hr.at[h], snd.at[3], rcv.at[3], (s, other))

    columns = pl.ds(pl.multiple_of(x * HD, HD), HD)
    settle(hr.at[pl.ds(0, NH - 1)], rcv.at[3])
    hidden = residual[c, :, columns].astype(F32) + jnp.sum(hr[...].astype(F32), axis=0)
    hid[c] = hidden
    square = jnp.sum(hidden * hidden, axis=1, keepdims=True)
    halves = ((ga, pa, a2, a3, pa_sem, x, y, at_x, at_y), (gb, pb, b2, b3, pb_sem, y, x, at_y, at_x))
    ga[y, x, 0:32] = (hidden * gain[:, columns]).astype(BF16)
    spread = jnp.where(iota((NS, HD), 0) == iota((NS, HD), 1), square, 0.0)
    sqz[z] = jnp.sum(spread, axis=0, keepdims=True)
    own = ga.at[y, x, pl.ds(0, 32)]
    for p in range(1, NZ):
        there = (((z + NZ - APART[p]) % NZ) * NY + y, h)
        place = ga.at[y, x, pl.ds(p * 32, 32)] if p < 4 else gb.at[x, y, pl.ds((p - 4) * 32, 32)]
        send(own, place, snd.at[4], z_sem.at[p // 2], there)
    for d in (4, 3, 5, 2, 6, 1, 7):
        there = (((z + d) % NZ) * NY + y, h)
        send(sqz.at[z], sqz.at[z], snd.at[5], rcv.at[5], there)
    send(hid.at[c], hid.at[c], snd.at[6], rcv.at[6], partner)
    done = []

    def block(ref, outer, inner, w):
        return ref.at[outer, inner, pl.ds(w * 64, 64)]

    def pass_on(half, w, inner, n):
        full, _, _, last, _, _, outer, _, at_last = halves[half]
        here = block(full, outer, inner, w)
        for d in OUT:
            send(here, here, snd.at[9 + half], last.at[w, n, d - 1], at_last((outer + d) % 4))
        cross(half, w, outer, inner, n)

    def cross(half, w, outer, inner, n):
        full, other, _, _, sem, _, _, _, _ = halves[half]
        send(block(full, outer, inner, w), block(other, outer, inner, w), snd.at[11 + half], sem.at[w, n], partner)
        done.append((half, w, outer, inner, n))

    for w in range(2):
        for half in range(2):
            full, _, first, _, _, inner, outer, at_first, _ = halves[half]
            here = block(full, outer, inner, w)
            if half == 0 and w == 0:
                settle(own, z_sem.at[0])
            else:
                settle(here, z_sem.at[half * 2 + w])
            for d in OUT:
                send(here, here, snd.at[7 + half], first.at[w, d - 1], at_first((inner + d) % 4))
            pass_on(half, w, inner, 0)
    settle(sqz.at[pl.ds(0, NZ - 1)], rcv.at[5])
    sqx[x] = jnp.sum(sqz[...], axis=0)
    for d in RING:
        send(sqx.at[x], sqx.at[x], snd.at[13], rcv.at[7], at_x((x + d) % NX))

    loads[2].wait()
    loads[3].wait()

    def multiply(items, sums):
        for half, w, outer, inner, n in items:
            full, other, _, _, sem, _, _, _, _ = halves[half]
            settle(block(other, outer, inner, w), sem.at[w, n])
        gate, up = sums
        for half, w, outer, inner, n in items:
            full, other, _, _, _, _, _, _, _ = halves[half]
            yy, xx = (inner, outer) if half else (outer, inner)
            both = (2 * w, 2 * w + 1)
            stream = jnp.concatenate(
                [
                    jnp.concatenate([ref[outer, inner, p * 32 : (p + 1) * 32] for p in both], axis=1)
                    for ref in (full, other)
                ],
                axis=0,
            )
            zs = [(z + APART[half * 4 + p]) % NZ for p in both]
            where = [pl.ds(pl.multiple_of(zz * 2048 + yy * 512 + xx * HD, HD), HD) for zz in zs]
            left = [jnp.concatenate([ref[:, at] for at in where], axis=1) for ref in (wg, wu)]
            gate = gate + lax.dot_general(left[0], stream, NT, preferred_element_type=F32)
            up = up + lax.dot_general(left[1], stream, NT, preferred_element_type=F32)
        return gate, up

    def catch_up(lag, batch, sums):
        while len(done) >= lag + batch:
            sums = multiply([done.pop(0) for _ in range(batch)], sums)
        return sums

    sums = (jnp.zeros((104, 64), F32), jnp.zeros((104, 64), F32))

    def last_arrivals(w, half, n, k):
        full, _, _, last, _, inner, outer, _, _ = halves[half]
        for d in RING:
            there, beside = (outer + 4 - d) % 4, (inner + 4 - k) % 4
            settle(block(full, there, beside, w), last.at[w, n, d - 1])
            cross(half, w, there, beside, 3 * n + 3 + d)

    for w in range(2):
        for half in range(2):
            full, _, first, _, _, inner, outer, _, _ = halves[half]
            for n, d in enumerate(RING):
                beside = (inner + 4 - d) % 4
                settle(block(full, outer, beside, w), first.at[w, d - 1])
                pass_on(half, w, beside, n + 1)
        for half in range(2):
            last_arrivals(w, half, 0, 0)
    settle(sqx.at[pl.ds(0, NX - 1)], rcv.at[7])
    sqy[y] = jnp.sum(sqx[...], axis=0)
    for d in RING:
        send(sqy.at[y], sqy.at[y], snd.at[14], rcv.at[8], at_y((y + d) % NY))
    sums = catch_up(LAG, BATCH, sums)
    for w in range(2):
        for n, k in enumerate(RING):
            for half in range(2):
                last_arrivals(w, half, n + 1, k)
                sums = catch_up(LAG, BATCH, sums)
        if w == 0:
            settle(sqy.at[pl.ds(0, NY - 1)], rcv.at[8])
            sqp[0] = jnp.sum(sqy[...], axis=0)
            send(sqp.at[0], sqp.at[1], snd.at[15], rcv.at[9], partner)
    sums = catch_up(LAST_BATCH, BATCH, sums)
    while done:
        sums = catch_up(0, min(LAST_BATCH, len(done)), sums)
    settle(sqp.at[0], rcv.at[9])
    square = jnp.broadcast_to(sqp[0], (8, HD)) + pltpu.roll(jnp.broadcast_to(sqp[1], (8, HD)), 32, 1)
    scale = lax.rsqrt(square[0:1, 0:64] * (1.0 / 16384.0) + EPSILON)
    gate = sums[0] * scale
    up = sums[1] * scale
    activation = (gate / (1.0 + jnp.exp(-gate)) * up).T.astype(BF16)

    loads[4].wait()
    turn = (2, 1, 3, 0)
    spots = [[(y + b) % NY, (x + b) % NX] for b in turn]

    def groups(r):
        k, first = r % 4, r // 4 * 4
        return [(spots[b][0], spots[k][1], first) for b in range(4)] + [
            (spots[k][0], spots[b][1], first + 2) for b in range(4)
        ]

    def down(r):
        for m, (yy, xx, first) in enumerate(groups(r)):
            weight = jnp.concatenate(
                [
                    wd[:, pl.ds(pl.multiple_of((first + zz) * 2048 + yy * 512 + xx * HD, HD), HD)]
                    for zz in range(2)
                ],
                axis=1,
            )
            product = jnp.dot(activation, weight, preferred_element_type=F32)
            for zz in range(2):
                at = slice(m * 64 + zz * 32, m * 64 + (zz + 1) * 32)
                piece = product[:, zz * HD : (zz + 1) * HD]
                o1[r, at] = piece[0:32]
                sb[r, at] = piece[32:64].astype(BF16)
        send(sb.at[r], rb.at[r], snd.at[16], rb_sem.at[r], partner)

    def finish(r):
        settle(rb.at[r], rb_sem.at[r])
        for half in range(2):
            for b in range(4):
                at = slice((half * 4 + b) * 64, (half * 4 + b + 1) * 64)
                whole = o1[r, at] + rb[r, at].astype(F32)
                if b == 3:
                    t1[r, half] = whole
                else:
                    s1[r, half * 3 + b] = whole.astype(BF16)
                    there = at_x(spots[b][1]) if half else at_y(spots[b][0])
                    send(s1.at[r, half * 3 + b], r1.at[r, half * 3 + b], snd.at[17], r1_sem.at[r], there)

    def reduce_one(r):
        k = r % 4
        settle(r1.at[r], r1_sem.at[r])
        low = iota((16, HD), 1) < 64
        for half in range(2):
            whole = t1[r, half]
            for b in range(3):
                whole = whole + r1[r, half * 3 + b].astype(F32)
            for zz in range(2):
                top, bottom = whole[zz * 32 : zz * 32 + 16], whole[zz * 32 + 16 : zz * 32 + 32]
                fs[r, half, zz, 0] = jnp.where(low, top, pltpu.roll(bottom, 64, 1)).astype(BF16)
                fs[r, half, zz, 1] = jnp.where(low, pltpu.roll(top, 64, 1), bottom).astype(BF16)
            yy, xx = (spots[k][0], x) if half else (y, spots[k][1])
            for zz in range(2):
                owner_z = r // 4 * 4 + half * 2 + zz
                for cc in range(2):

                    def go(zz=zz, cc=cc, owner_z=owner_z):
                        send(
                            fs.at[r, half, zz, cc],
                            fr.at[(c * NZ + z) * 4 + k],
                            snd.at[18],
                            rcv.at[10],
                            (owner_z * NY + yy, xx * NC + cc),
                        )

                    if k == 3:
                        pl.when((owner_z != z) | (cc != c))(go)
                    else:
                        go()

    for r in range(8):
        down(r)
        if r >= 2:
            finish(r - 2)
    for r in range(6, 8):
        finish(r)
    for r in range(4):
        reduce_one(r)
    for r in range(4, 8):
        reduce_one(r)
    fr[(c * NZ + z) * 4 + 3] = fs[z // 4 * 4 + 3, z % 4 // 2, z % 2, c]
    settle(hid.at[0], rcv.at[6])
    settle(fr.at[pl.ds(0, 63)], rcv.at[10])
    for t in range(2):
        added = jnp.sum(fr[t * 32 : (t + 1) * 32].astype(F32), axis=0)
        base = jnp.where(c == 0, hid[t, :, :64], hid[t, :, 64:])
        out[t, 0:16] = base[0:16] + added[:, :64]
        out[t, 16:32] = base[16:32] + added[:, 64:]

    for like, n in (
        (qall.at[pl.ds(0, NS - 1)], 0),
        (ps.at[pl.ds(0, NS - 1)], 1),
        (ss.at[pl.ds(0, NS - 1)], 20),
        (ag.at[pl.ds(0, NS - 1)], 2),
        (hp.at[pl.ds(0, NH - 1)], 3),
        (kv.at[pl.ds(0, 112)], 4),
        (sqz.at[pl.ds(0, NZ - 1)], 5),
        (hid.at[0], 6),
        (ga.at[0, pl.ds(0, 3)], 7),
        (gb.at[0, pl.ds(0, 3)], 8),
        (ga.at[pl.ds(0, 3)], 9),
        (gb.at[pl.ds(0, 3)], 10),
        (ga, 11),
        (gb, 12),
        (sqx.at[pl.ds(0, NX - 1)], 13),
        (sqy.at[pl.ds(0, NY - 1)], 14),
        (sqp.at[0], 15),
        (sb, 16),
        (s1, 17),
        (fr.at[pl.ds(0, 63)], 18),
    ):
        settle(like, snd.at[n])


def shards(
    lengths,
    block_table,
    slot_request,
    kv_pool,
    new_kv,
    queries,
    residual,
    norm_gain,
    w_out,
    w_gate,
    w_up,
    w_down,
):
    vmem = pl.BlockSpec(memory_space=pltpu.VMEM)
    anywhere = pl.BlockSpec(memory_space=pl.ANY)
    scratch = [
        ((3, 256), BF16),
        ((2, 1024), BF16),
        ((NS, 256), jnp.int32),
        ((2, NS, 512), BF16),
        ((1, 512), F32),
        ((TOKENS, 256), BF16),
        ((TOKENS, HD), BF16),
        ((1024, 512), BF16),
        ((104, 16384), BF16),
        ((104, 16384), BF16),
        ((104, 16384), BF16),
        ((NS, ROWS, HD), BF16),
        ((NS * ROWS, HD), BF16),
        ((PAGE, HD), F32),
        ((NS * ROWS, TOKENS), F32),
        ((NS * ROWS, HD), F32),
        ((NS * ROWS, 256), F32),
        ((NS, ROWS, HD), BF16),
        ((NS, ROWS, HD), BF16),
        ((NS, 1, HD), F32),
        ((NS, 1, HD), F32),
        ((NS, ROWS, HD), BF16),
        ((NS * ROWS, HD), F32),
        ((NH, 32, HD), BF16),
        ((NH, 32, HD), BF16),
        ((2, 32, HD), F32),
        ((NZ, 1, HD), F32),
        ((NX, 1, HD), F32),
        ((NY, 1, HD), F32),
        ((2, 1, HD), F32),
        ((NY, NX, 128, HD), BF16),
        ((NX, NY, 128, HD), BF16),
        ((NY, NX, 128, HD), BF16),
        ((NX, NY, 128, HD), BF16),
        ((8, 512, HD), F32),
        ((8, 512, HD), BF16),
        ((8, 512, HD), BF16),
        ((8, 6, 64, HD), BF16),
        ((8, 6, 64, HD), BF16),
        ((8, 2, 64, HD), F32),
        ((8, 2, 2, 2, 16, HD), BF16),
        ((64, 16, HD), BF16),
    ]
    return pl.pallas_call(
        kernel,
        out_shape=jax.ShapeDtypeStruct((2, NS, 64), F32),
        in_specs=[anywhere] * 12,
        out_specs=vmem,
        scratch_shapes=[pltpu.SMEM((NS,), jnp.int32)] * 2
        + [pltpu.VMEM(shape, kind) for shape, kind in scratch]
        + [
            pltpu.SemaphoreType.DMA(n)
            for n in ((12,), (21,), (15,), (4,), (2, 3), (2, 3), (2, 4, 3), (2, 4, 3), (2, 16), (2, 16), (8,), (8,))
        ],
        compiler_params=pltpu.CompilerParams(
            collective_id=0, has_side_effects=True, vmem_limit_bytes=56 * 1024 * 1024
        ),
    )(
        lengths,
        slot_request,
        new_kv.reshape(3, 256),
        queries.reshape(2, 1024),
        block_table,
        residual,
        norm_gain.reshape(1, 512),
        kv_pool.reshape(TOKENS, 256),
        w_out.reshape(1024, 512),
        w_gate,
        w_up,
        w_down,
    ).astype(BF16)


def solution(mesh):
    in_specs = (
        P(),
        P(),
        P(),
        P("seq", None, "head", None),
        P(None, "seq", "head", None),
        P(None, "seq", "head", None),
        P(None, None, "seq"),
        P("seq"),
        P("head", None, "seq"),
        P(("seq", "head"), None),
        P(("seq", "head"), None),
        P(("seq", "head"), None),
    )
    out_specs = P(None, None, ("seq", "head"))
    return jax.shard_map(shards, mesh=mesh, in_specs=in_specs, out_specs=out_specs, check_vma=False)
```
